512 devices in a mesh: dp: 128 (over z, y, core), mp: 4 (over x).
Axes of the slice: x: 4, y: 4, z: 16, core: 2. Of those that a mesh axis runs over, the one named last changes fastest.
Arguments:
- covariates: bfloat16 [262144, 512], P('dp', 'mp'), may hold values from -6 to 6
- weight: float32 [512, 256], P(None, 'mp'), may hold values from -0.25 to 0.25
- scale: float32 [4, 256], P(None, 'mp'), may hold values from 0.3 to 1.5
- z_lane: float32 [8192, 256], P('dp', 'mp'), may hold values from -6 to 6
- z_supplier: float32 [4096, 256], P('dp', 'mp'), may hold values from -6 to 6
- z_region: float32 [64, 256], P(None, 'mp'), may hold values from -6 to 6
- z_company: float32 [8, 256], P(None, 'mp'), may hold values from -6 to 6
- group_owner: int32 [8192, 1], P('dp'), may hold values from 0 to 127; in each aligned block of 64 rows (0 to 63, 64 to 127, ...) at most 2 rows name the same one
- group_local: int32 [8192], P('dp'), may hold values from 0 to 63
- group_len: int32 [8192], P('dp'), may hold values from 1 to 32, 157286 in all
- event_bin: int32 [262144], P('dp'), may hold values from 0 to 255
- observed: int32 [262144], P('dp'), may hold values 0 or 1
- lane_supplier: int32 [8192], P('dp'), may hold values from 0 to 4095
- supplier_region: int32 [4096], replicated, may hold values from 0 to 63
- region_company: int32 [64], replicated, may hold values from 0 to 7
Outputs:
- grad_weight: float32 [512, 256], P(None, 'mp')
- grad_lane: float32 [8192, 256], P('dp', 'mp')
- grad_supplier: float32 [4096, 256], P('dp', 'mp')
- grad_region: float32 [64, 256], P(None, 'mp')
- grad_company: float32 [8, 256], P(None, 'mp')
- grad_scale: float32 [4, 256], P(None, 'mp')
The draws below stay inside these ranges and needn't reach their ends.
Inputs may be any that keep to these rules, and one draw needn't show every extreme that they name: `group_owner`: among the 64 groups of one index of dp no owner is named more than 2 times, a bound that some block reaches.
All inputs are finite; a program needn't handle non-finite values. No bound on the sum of `group_len` or of `observed` on one device may be relied on, other than what follows from the above.
Results may differ from the reference program's by a relative error of at most 0.003.
Values may be sent and summed in bfloat16 or wider, within the bound.
A program may use at most 64 MiB of HBM per device.

```python
import math
import jax
import jax.numpy as jnp
import numpy as np
from jax import lax

COV = 512
NBIN = 256
GS = 32
GD = 64
LANE_DEV = 64
RG = 64
CO = 8
CAP = 2
GROUPS = 8192
SHIP = 262144
LANES = 8192
SUPPLIERS = 4096
N_DP = 128


def plant(values, key, low, top_value):
    shape = values.shape
    spot = [jax.random.randint(jax.random.fold_in(key, axis), (), 0, shape[axis]) for axis in range(len(shape))]
    values = values.at[tuple(spot)].set(low)
    longest = shape.index(max(shape))
    spot[longest] = (spot[longest] + 1) % shape[longest]
    return values.at[tuple(spot)].set(top_value)


def block_scale(own_key, shape, pieces, smallest, top_value):
    loudness = 1.0
    for axis_at, shards_of in pieces:
        steps = jax.random.uniform(jax.random.fold_in(jax.random.fold_in(own_key, 6), axis_at), (shards_of,), jnp.float32, smallest / len(pieces), top_value / len(pieces))
        loudness = loudness * jnp.repeat(jnp.exp(steps), shape[axis_at] // shards_of).reshape((-1,) + (1,) * (len(shape) - 1 - axis_at))
    return loudness


def split_up(number_of, total, bound, skew):
    loads = [(1 << 20) // math.isqrt(grade ** skew) + 1 for grade in range(2, number_of + 1)]
    spare, given = total - bound - (number_of - 1), [1] * (number_of - 1)
    while spare > 0:
        free = [i for i in range(number_of - 1) if given[i] < bound]
        mass, remaining = sum([loads[i] for i in free]), spare
        for i in free:
            more = min(bound - given[i], max(1, remaining * loads[i] // mass), spare)
            given[i] = given[i] + more
            spare = spare - more
    return np.array([bound] + given)


def uneven_parts(rng, amount, total, most, skew):
    if amount == 2:
        one = jax.random.randint(rng, (), max(1, total - most), min(most, total - 1) + 1)
        return jnp.stack([one, total - one])
    tallies = jnp.asarray(split_up(amount, total, most, skew), jnp.int32)
    couples = (amount - 1) // 2
    donor, receiver = tallies[1:1 + 2 * couples:2], tallies[2:2 + 2 * couples:2]
    slack = jnp.minimum(donor - 1, most - receiver)
    moved = jax.random.randint(jax.random.fold_in(rng, 1), (couples,), 0, 1 << 20) % (slack + 1)
    tallies = tallies.at[1:1 + 2 * couples:2].set(donor - moved).at[2:2 + 2 * couples:2].set(receiver + moved)
    return tallies[jax.random.permutation(jax.random.fold_in(rng, 2), amount)]


def assign_block(stream_key, own, number, rows, amount, top, most, lean):
    sequence = jax.random.permutation(stream_key, amount)
    packed, common = portions_of(amount, rows * top, most, lean, True), portions_of(amount, rows * top, most, lean, False)
    places = jnp.arange(amount)

    def named(sizes, offset_by):
        used = int((sizes > 0).sum())
        fixed = max(1, used // 4)
        passed = fixed + (places - fixed + offset_by * (used - fixed)) % max(1, amount - fixed)
        return jnp.zeros((amount,), jnp.int32).at[sequence[jnp.where(places < fixed, places, passed)]].set(jnp.asarray(sizes, jnp.int32))

    sizes = jnp.where(number % 4 == 0, named(packed, number // 4), named(common, number - number // 4 - 1))
    mixed = jax.random.permutation(jax.random.fold_in(own, 3), amount)
    donor, taker = mixed[0:amount // 2 * 2:2], mixed[1:amount // 2 * 2:2]
    margin = jnp.minimum(sizes[donor] - 1, most - sizes[taker]) // 2
    margin = jnp.where((donor == sequence[0]) | (taker == sequence[0]) | (sizes[taker] == 0), 0, jnp.maximum(margin, 0))
    passed = jax.random.randint(jax.random.fold_in(own, 4), (amount // 2,), 0, 1 << 20) % (margin + 1)
    sizes = sizes.at[donor].add(-passed).at[taker].add(passed)
    items = jnp.searchsorted(jnp.cumsum(sizes), jnp.arange(rows * top), side="right").astype(jnp.int32)
    table = items.reshape(top, rows).T
    table = table[jax.random.permutation(jax.random.fold_in(own, 1), rows)]
    offset_by = jax.random.randint(jax.random.fold_in(own, 2), (rows, 1), 0, top)
    return jnp.take_along_axis(table, (jnp.arange(top)[None, :] + offset_by) % top, axis=1)


def portions_of(count, total, most, lean, full):
    loads = [(1 << 20) // math.isqrt(standing ** lean) + 1 for standing in range(1, count + 1)]
    largest = most if full else min(most, max(-(-total // count), total * loads[0] // sum(loads)))
    least = 1 if total - largest >= count - 1 else 0
    counts, surplus = [largest] + [least] * (count - 1), total - largest - least * (count - 1)
    while surplus > 0:
        free = [i for i in range(1, count) if counts[i] < largest] or [i for i in range(1, count) if counts[i] < most]
        whole, remaining = sum([loads[i] for i in free]), surplus
        for i in free:
            extra = min(most - counts[i], max(1, remaining * loads[i] // whole), surplus)
            counts[i] = counts[i] + extra
            surplus = surplus - extra
    return np.array(counts)


def normal_values(stream_key, extent, scale, limit, shards=(), kind=jnp.bfloat16):
    drawn = scale * jax.random.normal(stream_key, extent, jnp.float32)
    if shards:
        drawn = drawn * block_scale(stream_key, extent, shards, -0.22, 0.18)
    return jnp.clip(drawn, -limit, limit).astype(kind)


def setup_inputs(seed: int = 0) -> dict:
    key_of = jax.random.split(jax.random.key(seed), 16)
    covariates = normal_values(key_of[0], (SHIP, COV), 1.0, 6.0, ((0, 128), (1, 4)))
    weight = normal_values(key_of[1], (COV, NBIN), COV ** -0.5, 0.25, ((1, 4),), jnp.float32)
    scale = jnp.clip(jnp.exp(math.log(1.5) - 1.60943787 * jax.random.uniform(key_of[2], (4, NBIN), jnp.float32) ** block_scale(key_of[2], (4, NBIN), ((1, 4),), -0.2, 0.2)), 0.3, 1.5)
    z_lane = normal_values(key_of[3], (LANES, NBIN), 1.0, 6.0, ((0, 128), (1, 4)), jnp.float32)
    z_supplier = normal_values(key_of[4], (SUPPLIERS, NBIN), 1.0, 6.0, ((0, 128), (1, 4)), jnp.float32)
    z_region = normal_values(key_of[5], (RG, NBIN), 1.0, 6.0, ((1, 4),), jnp.float32)
    z_company = normal_values(key_of[6], (CO, NBIN), 1.0, 6.0, ((1, 4),), jnp.float32)
    group_owner_keys = jax.random.split(jax.random.fold_in(key_of[7], 1), GROUPS // GD)
    group_owner_turns = jax.random.permutation(jax.random.fold_in(key_of[7], 3), GROUPS // GD)
    group_owner = jax.vmap(lambda own, number: assign_block(jax.random.fold_in(key_of[7], 2), own, number, GD, N_DP, 1, CAP, 2))(group_owner_keys, group_owner_turns).reshape((GROUPS, 1))
    group_local = plant(jax.random.randint(key_of[8], (GROUPS,), 0, LANE_DEV), jax.random.fold_in(key_of[8], 1), 0, LANE_DEV - 1).astype(jnp.int32)
    group_len = uneven_parts(key_of[9], GROUPS, GROUPS * GS * 3 // 5, GS, 2).astype(jnp.int32)
    event_bin = plant(jax.random.randint(key_of[10], (SHIP,), 0, NBIN), jax.random.fold_in(key_of[10], 1), 0, NBIN - 1).astype(jnp.int32)
    observed = plant((jax.random.randint(key_of[11], (SHIP,), 0, 5) < 3).astype(jnp.int32), jax.random.fold_in(key_of[11], 1), 0, 1)
    lane_supplier = plant(jax.random.randint(key_of[12], (LANES,), 0, SUPPLIERS), jax.random.fold_in(key_of[12], 1), 0, SUPPLIERS - 1).astype(jnp.int32)
    supplier_region = plant(jax.random.randint(key_of[13], (SUPPLIERS,), 0, RG), jax.random.fold_in(key_of[13], 1), 0, RG - 1).astype(jnp.int32)
    region_company = plant(jax.random.randint(key_of[14], (RG,), 0, CO), jax.random.fold_in(key_of[14], 1), 0, CO - 1).astype(jnp.int32)
    return dict(covariates=covariates, weight=weight, scale=scale, z_lane=z_lane, z_supplier=z_supplier, z_region=z_region, z_company=z_company, group_owner=group_owner, group_local=group_local, group_len=group_len, event_bin=event_bin, observed=observed, lane_supplier=lane_supplier, supplier_region=supplier_region, region_company=region_company)


def reference(covariates, weight, scale, z_lane, z_supplier, z_region, z_company, group_owner, group_local, group_len, event_bin, observed, lane_supplier, supplier_region, region_company):
    company_effect = scale[0] * z_company
    region_effect = scale[1] * z_region + company_effect[region_company]
    supplier_path = scale[2] * z_supplier + region_effect[supplier_region]
    lane_offset = (scale[3] * z_lane + supplier_path[lane_supplier]).astype(jnp.bfloat16)
    lane_id = (group_owner[:, 0] * LANE_DEV + group_local).astype(jnp.int32)
    group_offset = lane_offset[lane_id].astype(jnp.float32)
    linear = jnp.dot(covariates, weight.astype(jnp.bfloat16), preferred_element_type=jnp.float32)
    eta = linear.reshape(GROUPS, GS, NBIN) + group_offset[:, None, :]
    hazard = jax.nn.sigmoid(eta)
    bins = jnp.arange(NBIN, dtype=jnp.int32)[None, None, :]
    events = event_bin.reshape(GROUPS, GS, 1)
    flags = observed.reshape(GROUPS, GS, 1).astype(jnp.float32)
    live = (jnp.arange(GS, dtype=jnp.int32)[None, :] < group_len[:, None]).astype(jnp.float32)[:, :, None]
    score = live * jnp.where(bins < events, -hazard, jnp.where(bins == events, flags - hazard, jnp.float32(0.0)))
    score_rows = score.reshape(SHIP, NBIN).astype(jnp.bfloat16)
    weight_sum = lax.dot_general(covariates, score_rows, (((0,), (0,)), ((), ())), preferred_element_type=jnp.float32)
    group_sum = jnp.sum(score, axis=1)
    lane_total = jax.ops.segment_sum(group_sum, lane_id, num_segments=LANES)
    supplier_total = jax.ops.segment_sum(lane_total, lane_supplier, num_segments=SUPPLIERS)
    region_total = jax.ops.segment_sum(supplier_total, supplier_region, num_segments=RG)
    company_total = jax.ops.segment_sum(region_total, region_company, num_segments=CO)
    grad_scale = jnp.stack([
        jnp.sum(z_company * company_total, axis=0),
        jnp.sum(z_region * region_total, axis=0),
        jnp.sum(z_supplier * supplier_total, axis=0),
        jnp.sum(z_lane * lane_total, axis=0)])
    return (weight_sum - weight,
            scale[3] * lane_total - z_lane,
            scale[2] * supplier_total - z_supplier,
            scale[1] * region_total - z_region,
            scale[0] * company_total - z_company,
            grad_scale)
```

```python
import jax
import jax.numpy as jnp
from jax import lax
from jax.experimental import pallas as pl
from jax.experimental.pallas import tpu as pltpu
from jax.sharding import PartitionSpec as P

HIGHEST = lax.Precision.HIGHEST
F = jnp.float32
B = jnp.bfloat16
I = jnp.int32
CHUNKS = 4
ROWS = 2048
CH = ROWS // CHUNKS
HALF = CH // 2


def iota(shape, axis):
    return lax.broadcasted_iota(I, shape, axis)


def mm(a, b, ca=1, cb=0, precision=None):
    return lax.dot_general(
        a, b, (((ca,), (cb,)), ((), ())), preferred_element_type=F, precision=precision
    )


def pick(cond, dtype=F):
    return jnp.where(cond, jnp.float32(1.0), jnp.float32(0.0)).astype(dtype)


def column(row):
    n = row.shape[1]
    return jnp.sum(
        jnp.where(iota((n, n), 0) == iota((n, n), 1), row, jnp.zeros_like(row)),
        axis=1,
        keepdims=True,
    )


def row_of(col):
    n = col.shape[0]
    return jnp.sum(
        jnp.where(iota((n, n), 0) == iota((n, n), 1), col, jnp.zeros_like(col)),
        axis=0,
        keepdims=True,
    )


def side(a, b):
    return jnp.concatenate([a, b], axis=1)


def split(value):
    high = value.astype(B)
    low = (value - high.astype(F)).astype(B)
    return side(high, low)


def kernel(
    cov,
    weight,
    scale,
    z_lane,
    z_supplier,
    z_region,
    z_company,
    group_owner,
    group_local,
    group_len,
    event_bin,
    observed,
    lane_supplier,
    supplier_region,
    region_company,
    grad_weight,
    grad_lane,
    grad_supplier,
    grad_region,
    grad_company,
    grad_scale,
    covers,
    linear,
    scores,
    nodes,
    lane_ids,
    group_ids,
    found_ids,
    row_ids,
    reply,
    replied,
    sums,
    parts,
    parted,
    part_in,
    far_in,
    near_in,
    near_lane,
    whole,
    local_sem,
    send_sem,
    recv_sem,
):
    dp = lax.axis_index("dp")
    mp = lax.axis_index("mp")
    z = lax.div(dp, 8)
    yc = lax.rem(dp, 8)
    r = lax.rem(z, 4)
    q = lax.div(z, 4)
    right = lax.rem(mp + 1, 4)
    left = lax.rem(mp + 3, 4)

    def at_z(step):
        return {"dp": lax.rem(z + step, 16) * 8 + yc, "mp": mp}

    def at_yc(step):
        return {"dp": z * 8 + lax.rem(yc + step, 8), "mp": mp}

    def at_x(index):
        return {"dp": dp, "mp": index}

    count = [0]
    started = []

    def send(src, dst, device):
        slot = count[0]
        count[0] = slot + 1
        copy = pltpu.make_async_remote_copy(
            src_ref=src,
            dst_ref=dst,
            send_sem=send_sem.at[slot],
            recv_sem=recv_sem.at[slot],
            device_id=device,
            device_id_type=pl.DeviceIdType.MESH,
        )
        copy.start()
        started.append(copy)
        return copy

    def arrive(copies):
        for copy in copies:
            copy.wait_recv()

    def far(buf):
        return [send(buf.at[r, q], buf.at[r, q], at_z(step)) for step in (4, 12, 8)]

    def near(buf):
        return [
            send(buf.at[r], buf.at[r], at_z(1)),
            send(buf.at[r], buf.at[r], at_z(15)),
            send(buf.at[r, pl.ds(0, 2)], buf.at[r, pl.ds(0, 2)], at_z(2)),
            send(buf.at[r, pl.ds(2, 2)], buf.at[r, pl.ds(2, 2)], at_z(14)),
        ]

    def plane(buf):
        return [send(buf.at[yc], buf.at[yc], at_yc(step)) for step in range(1, 8)]

    def scatter(source, target):
        return [
            send(source.at[lax.rem(yc + step, 8)], target.at[yc], at_yc(step))
            for step in range(1, 8)
        ]

    barrier = pltpu.get_barrier_semaphore()
    partners = [at_yc(step) for step in range(1, 8)]
    partners += [at_z(step) for step in (1, 2, 4, 8, 12, 14, 15)]
    partners += [at_x(right), at_x(left)]
    for device in partners:
        pl.semaphore_signal(
            barrier, inc=1, device_id=device, device_id_type=pl.DeviceIdType.MESH
        )

    own_owner = row_of(group_owner[...].astype(F))
    own_local = group_local[...].astype(F)
    nodes[r, q, 0:64, :] = split(z_lane[...])
    nodes[r, q, 64:96, :] = split(z_supplier[...])
    lane_ids[r, q] = side(lane_supplier[...].astype(F), jnp.zeros((1, 64), F))
    group_ids[yc] = side(own_owner, own_local)
    pl.semaphore_wait(barrier, len(partners))

    chunk_rows = [pl.ds(c * CH, CH) for c in range(CHUNKS)]
    own_copies = []
    for c in range(CHUNKS):
        copy = pltpu.make_async_copy(
            cov.at[chunk_rows[c]], covers.at[mp, chunk_rows[c]], local_sem.at[c]
        )
        copy.start()
        own_copies.append(copy)
    group_id_copies = plane(group_ids)
    lane_id_copies = far(lane_ids)
    node_copies = far(nodes)
    direct = []
    for c in range(CHUNKS):
        block = covers.at[mp, chunk_rows[c]]
        direct.append(
            [
                send(cov.at[chunk_rows[c]], block, at_x(right)),
                send(cov.at[chunk_rows[c]], block, at_x(left)),
            ]
        )
    passed = []

    def forward(c):
        arrive(direct[c])
        first = covers.at[left, pl.ds(c * CH, HALF)]
        second = covers.at[right, pl.ds(c * CH + HALF, HALF)]
        passed.append([send(first, first, at_x(right)), send(second, second, at_x(left))])

    weight_rows = weight[...].T.astype(B)
    company_effect = scale[0:1, :] * z_company[...]
    companies = region_company[...]
    company_pick = pick(iota((64, 8), 1) == column(companies.astype(F)).astype(I))
    region_effect = scale[1:2, :] * z_region[...] + mm(
        company_pick, company_effect, precision=HIGHEST
    )
    lens = group_len[...].astype(F)
    spread = jnp.where(
        (iota((16, 64), 1) >> 2) == iota((16, 64), 0), lens, jnp.zeros_like(lens)
    )
    lanes_of = pick((iota((64, 128), 0) & 3) == (iota((64, 128), 1) >> 5), B)
    live_len = mm(spread.astype(B), lanes_of).astype(I)
    ends = jnp.where((iota((16, 128), 1) & 31) < live_len, event_bin[...], -1)
    flags = observed[...].astype(F)

    arrive(lane_id_copies)
    lane_id_copies = near(lane_ids)
    arrive(node_copies)
    node_copies = near(nodes)
    forward(0)

    arrive(group_id_copies)
    ids = jnp.concatenate([group_ids[j] for j in range(8)], axis=0).astype(I)
    owners, locals_ = ids[:, 0:64], ids[:, 64:128]
    owner_z = owners >> 3
    held = jnp.where((owners & 7) == yc, (owner_z & 3) * 4 + (owner_z >> 2), -1)
    lane_key = jnp.where(held >= 0, held * 64 + locals_, -1)

    arrive(lane_id_copies)
    table = jnp.concatenate([lane_ids[a, b] for a in range(4) for b in range(4)], axis=0)
    table = table.T[0:64, :]
    found = []
    for j in range(8):
        of_owner = mm(table, pick(iota((16, 64), 0) == held[j : j + 1, :]), precision=HIGHEST)
        found.append(
            jnp.sum(
                jnp.where(
                    iota((64, 64), 0) == locals_[j : j + 1, :], of_owner, jnp.float32(0.0)
                ),
                axis=0,
                keepdims=True,
            )
        )
    found = jnp.concatenate(found, axis=0)
    found_ids[yc] = side(found, jnp.zeros((8, 64), F))
    found_copies = plane(found_ids)
    forward(1)

    lane_columns = [
        column(lane_key[j : j + 1, :].astype(F)).astype(I) for j in range(8)
    ]

    arrive(found_copies)
    suppliers = found_ids[0]
    for j in range(1, 8):
        suppliers = suppliers + found_ids[j]
    suppliers = suppliers[:, 0:64]
    own_supplier = jnp.sum(
        jnp.where(iota((8, 64), 0) == yc, suppliers, jnp.float32(0.0)), axis=0, keepdims=True
    )
    row_ids[r, q] = side(own_supplier, own_owner * 64.0 + own_local)
    row_id_copies = far(row_ids)
    suppliers = suppliers.astype(I)
    sup_owner = suppliers >> 5
    sup_z = sup_owner >> 3
    sup_key = jnp.where(
        (sup_owner & 7) == yc,
        ((sup_z & 3) * 4 + (sup_z >> 2)) * 32 + (suppliers & 31),
        -1,
    )
    forward(2)

    own_sup_col = column(own_supplier).astype(I)
    sup_row = pick(iota((64, 32), 1) == (own_sup_col >> 7), B)
    region_table = mm(sup_row, supplier_region[...].astype(F).astype(B))
    group_region = jnp.sum(
        jnp.where(iota((64, 128), 1) == (own_sup_col & 127), region_table, jnp.float32(0.0)),
        axis=1,
        keepdims=True,
    )
    region_col = group_region.astype(I)
    region_row = row_of(group_region).astype(I)
    group_effect = mm(
        pick(iota((64, 64), 1) == region_col), region_effect, precision=HIGHEST
    )
    arrive(row_id_copies)
    row_id_copies = near(row_ids)

    arrive(node_copies)
    lane_nodes = nodes[:, :, 0:64, :].reshape(1024, 128)
    sup_nodes = nodes[:, :, 64:96, :].reshape(512, 128)
    for j in range(8):
        lane_pick = pick(iota((64, 1024), 1) == lane_columns[j], B)
        sup_col = column(sup_key[j : j + 1, :].astype(F)).astype(I)
        sup_pick = pick(iota((64, 512), 1) == sup_col, B)
        reply[j, 0] = mm(lane_pick, lane_nodes).astype(B)
        reply[j, 1] = mm(sup_pick, sup_nodes).astype(B)
    replied[yc] = reply[yc]
    reply_copies = scatter(reply, replied)
    forward(3)

    arrive(row_id_copies)
    held_rows = jnp.concatenate(
        [row_ids[a, b] for a in range(4) for b in range(4)], axis=0
    ).astype(I)

    def along(start):
        return jnp.concatenate(
            [held_rows[k : k + 1, start : start + 32] for k in range(16)], axis=1
        )

    sup_along = side(along(0), along(32)) - z * 256
    lane_along = side(along(64), along(96)) - z * 512

    for c in range(CHUNKS):
        own_copies[c].wait()
        arrive(passed[c])
        rows = jnp.concatenate([covers[k, c * CH : (c + 1) * CH, :] for k in range(4)], axis=1)
        linear[:, c * CH : (c + 1) * CH] = mm(weight_rows, rows, 1, 1)

    arrive(reply_copies)
    got = replied[0].astype(F)
    for j in range(1, 8):
        got = got + replied[j].astype(F)
    lane_latent = got[0, :, 0:64] + got[0, :, 64:128]
    sup_latent = got[1, :, 0:64] + got[1, :, 64:128]
    path = scale[2:3, :] * sup_latent + group_effect
    offset = (scale[3:4, :] * lane_latent + path).astype(B)
    offset = offset.astype(F).T.astype(B)

    bins = iota((64, 128), 0) + mp * 64
    for s in range(16):
        at = slice(s * 128, (s + 1) * 128)
        expand = pick(iota((64, 128), 0) == (iota((64, 128), 1) >> 5) + 4 * s, B)
        eta = linear[:, at] + mm(offset, expand)
        hazard = jax.nn.sigmoid(eta)
        end = ends[s : s + 1, :]
        score = jnp.where(
            bins < end,
            -hazard,
            jnp.where(bins == end, flags[s : s + 1, :] - hazard, jnp.float32(0.0)),
        )
        scores[:, at] = score.astype(B)

    score_rows = scores[...]
    group_pick = pick(iota((64, 2048), 0) == (iota((64, 2048), 1) >> 5), B)
    group_sum = mm(group_pick, score_rows, 1, 1)
    sums[r, q] = side(group_sum[0:32, :], group_sum[32:64, :]).astype(B)
    sum_copies = far(sums)

    for pair in range(2):
        block = side(covers[2 * pair], covers[2 * pair + 1])
        product = mm(score_rows, block)
        for half in range(2):
            first = (2 * pair + half) * 64
            piece = product[:, half * 128 : (half + 1) * 128]
            done = 0
            while done < 64:
                where, inside = divmod(first + done, 40)
                size = min(40 - inside, 64 - done)
                parts[where, inside : inside + size, :] = piece[done : done + size, :]
                done += size
    by_region = mm(
        pick(iota((64, 64), 0) == region_row), group_sum, precision=HIGHEST
    )
    by_region = side(by_region[0:32, :], by_region[32:64, :])
    scale_part = side(
        jnp.sum(lane_latent * group_sum, axis=0, keepdims=True),
        jnp.sum(sup_latent * group_sum, axis=0, keepdims=True),
    )
    parts[6, 16:40, :] = by_region[0:24, :]
    parts[7, 0:8, :] = by_region[24:32, :]
    parts[7, 8:16, :] = jnp.where(iota((8, 128), 0) == 0, scale_part, jnp.float32(0.0))
    parts[7, 16:40, :] = jnp.zeros((24, 128), F)
    part_in[yc] = parts[yc]
    part_copies = scatter(parts, part_in)

    lane_hit = pick(iota((512, 1024), 0) == lane_along, B)
    sup_hit = pick(iota((256, 1024), 0) == sup_along, B)
    arrive(sum_copies)
    sum_copies = near(sums)
    arrive(part_copies)
    total = part_in[0]
    for j in range(1, 8):
        total = total + part_in[j]
    far_in[q] = total
    far_copies = [send(far_in.at[q], far_in.at[q], at_z(step)) for step in (4, 12, 8)]

    arrive(sum_copies)
    gathered = sums[...].reshape(512, 128)
    gathered = jnp.concatenate([gathered[:, 0:64], gathered[:, 64:128]], axis=0)
    by_lane = mm(lane_hit, gathered)
    by_supplier = mm(sup_hit, gathered)
    for j in range(8):
        parted[j, 0:32, :] = side(
            by_lane[j * 64 : j * 64 + 32, :], by_lane[j * 64 + 32 : j * 64 + 64, :]
        )
        parted[j, 32:48, :] = side(
            by_supplier[j * 32 : j * 32 + 16, :], by_supplier[j * 32 + 16 : j * 32 + 32, :]
        )
    near_lane[yc] = parted[yc]
    lane_copies = scatter(parted, near_lane)

    arrive(far_copies)
    near_in[r] = (far_in[0] + far_in[1]) + (far_in[2] + far_in[3])
    near_copies = [send(near_in.at[r], near_in.at[r], at_z(step)) for step in (1, 15, 2)]

    arrive(lane_copies)
    total = near_lane[0]
    for j in range(1, 8):
        total = total + near_lane[j]
    lane_total = jnp.concatenate([total[0:32, 0:64], total[0:32, 64:128]], axis=0)
    supplier_total = jnp.concatenate([total[32:48, 0:64], total[32:48, 64:128]], axis=0)
    grad_lane[...] = scale[3:4, :] * lane_total - z_lane[...]
    grad_supplier[...] = scale[2:3, :] * supplier_total - z_supplier[...]

    arrive(near_copies)
    whole[yc] = (near_in[0] + near_in[1]) + (near_in[2] + near_in[3])
    whole_copies = plane(whole)
    arrive(whole_copies)

    def whole_rows(first, size):
        pieces = []
        done = 0
        while done < size:
            where, inside = divmod(first + done, 40)
            step = min(40 - inside, size - done)
            pieces.append(whole[where, inside : inside + step, :])
            done += step
        return pieces[0] if len(pieces) == 1 else jnp.concatenate(pieces, axis=0)

    for k in range(4):
        at = slice(k * 128, (k + 1) * 128)
        grad_weight[at, :] = whole_rows(k * 64, 64).T - weight[at, :]
    by_region = whole_rows(256, 32)
    region_total = jnp.concatenate([by_region[:, 0:64], by_region[:, 64:128]], axis=0)
    scale_total = whole_rows(288, 8)[0:1, :]
    company_total = mm(
        pick(iota((8, 64), 0) == companies), region_total, precision=HIGHEST
    )
    grad_region[...] = scale[1:2, :] * region_total - z_region[...]
    grad_company[...] = scale[0:1, :] * company_total - z_company[...]
    grad_scale[0:1, :] = jnp.sum(z_company[...] * company_total, axis=0, keepdims=True)
    grad_scale[1:2, :] = jnp.sum(z_region[...] * region_total, axis=0, keepdims=True)
    grad_scale[2:3, :] = scale_total[:, 64:128]
    grad_scale[3:4, :] = scale_total[:, 0:64]

    for copy in started:
        copy.wait_send()


def per_device(
    covariates,
    weight,
    scale,
    z_lane,
    z_supplier,
    z_region,
    z_company,
    group_owner,
    group_local,
    group_len,
    event_bin,
    observed,
    lane_supplier,
    supplier_region,
    region_company,
):
    vmem = pl.BlockSpec(memory_space=pltpu.VMEM)
    slots = 160
    return pl.pallas_call(
        kernel,
        out_shape=(
            jax.ShapeDtypeStruct((512, 64), F),
            jax.ShapeDtypeStruct((64, 64), F),
            jax.ShapeDtypeStruct((32, 64), F),
            jax.ShapeDtypeStruct((64, 64), F),
            jax.ShapeDtypeStruct((8, 64), F),
            jax.ShapeDtypeStruct((4, 64), F),
        ),
        in_specs=[pl.BlockSpec(memory_space=pl.ANY)] + [vmem] * 14,
        out_specs=(vmem,) * 6,
        scratch_shapes=[
            pltpu.VMEM((4, ROWS, 128), B),
            pltpu.VMEM((64, ROWS), F),
            pltpu.VMEM((64, ROWS), B),
            pltpu.VMEM((4, 4, 96, 128), B),
            pltpu.VMEM((4, 4, 1, 128), F),
            pltpu.VMEM((8, 1, 128), F),
            pltpu.VMEM((8, 8, 128), F),
            pltpu.VMEM((4, 4, 1, 128), F),
            pltpu.VMEM((8, 2, 64, 128), B),
            pltpu.VMEM((8, 2, 64, 128), B),
            pltpu.VMEM((4, 4, 32, 128), B),
            pltpu.VMEM((8, 40, 128), F),
            pltpu.VMEM((8, 48, 128), F),
            pltpu.VMEM((8, 40, 128), F),
            pltpu.VMEM((4, 40, 128), F),
            pltpu.VMEM((4, 40, 128), F),
            pltpu.VMEM((8, 48, 128), F),
            pltpu.VMEM((8, 40, 128), F),
            pltpu.SemaphoreType.DMA((CHUNKS,)),
            pltpu.SemaphoreType.DMA((slots,)),
            pltpu.SemaphoreType.DMA((slots,)),
        ],
        compiler_params=pltpu.CompilerParams(
            collective_id=0, has_side_effects=True, vmem_limit_bytes=48 * 1024 * 1024
        ),
        name="hazard_gradient",
    )(
        covariates,
        weight,
        scale,
        z_lane,
        z_supplier,
        z_region,
        z_company,
        group_owner,
        group_local.reshape(1, 64),
        group_len.reshape(1, 64),
        event_bin.reshape(16, 128),
        observed.reshape(16, 128),
        lane_supplier.reshape(1, 64),
        supplier_region.reshape(32, 128),
        region_company.reshape(1, 64),
    )


def solution(mesh):
    in_specs = (
        P("dp", "mp"),
        P(None, "mp"),
        P(None, "mp"),
        P("dp", "mp"),
        P("dp", "mp"),
        P(None, "mp"),
        P(None, "mp"),
        P("dp", None),
        P("dp"),
        P("dp"),
        P("dp"),
        P("dp"),
        P("dp"),
        P(),
        P(),
    )
    out_specs = (
        P(None, "mp"),
        P("dp", "mp"),
        P("dp", "mp"),
        P(None, "mp"),
        P(None, "mp"),
        P(None, "mp"),
    )
    return jax.shard_map(
        per_device, mesh=mesh, in_specs=in_specs, out_specs=out_specs, check_vma=False
    )
```

```python
import jax
import jax.numpy as jnp
from jax import lax
from jax.experimental import pallas as pl
from jax.experimental.pallas import tpu as pltpu
from jax.sharding import PartitionSpec as P

HIGHEST = lax.Precision.HIGHEST
F = jnp.float32
B = jnp.bfloat16
I = jnp.int32
S = jnp.int16
VMEM_BYTES = 60 * 1024 * 1024
CHUNKS = 8
ROWS = 2048
CH = ROWS // CHUNKS
HALF = CH // 2
STEPS = (8, 7, 9, 6, 10, 5, 11, 4, 12, 3, 13, 2, 14, 1, 15)
UNIT = 5461.0


def iota(shape, axis):
    return lax.broadcasted_iota(I, shape, axis)


def mm(a, b, ca=1, cb=0, precision=None):
    return lax.dot_general(
        a, b, (((ca,), (cb,)), ((), ())), preferred_element_type=F, precision=precision
    )


def pick(cond, dtype=F):
    return jnp.where(cond, jnp.float32(1.0), jnp.float32(0.0)).astype(dtype)


def column(row):
    n = row.shape[1]
    return jnp.sum(
        jnp.where(iota((n, n), 0) == iota((n, n), 1), row, jnp.zeros_like(row)),
        axis=1,
        keepdims=True,
    )


def row_of(col):
    n = col.shape[0]
    return jnp.sum(
        jnp.where(iota((n, n), 0) == iota((n, n), 1), col, jnp.zeros_like(col)),
        axis=0,
        keepdims=True,
    )


def side(a, b):
    return jnp.concatenate([a, b], axis=1)


def fixed(value):
    return jnp.floor(value * UNIT + 0.5).astype(I)


def stack(value, rows):
    return jnp.concatenate([value[:rows, 0:64], value[:rows, 64:128]], axis=0)


def fold(value):
    half = value.shape[0] // 2
    return side(value[:half, :], value[half:, :])


def kernel(*refs):
    hbm = refs[:15]
    result = refs[15]
    held_in = refs[16:30]
    (
        covers,
        linear,
        scores,
        nodes,
        lane_ids,
        group_ids,
        found_ids,
        row_ids,
        reply,
        replied,
        sums,
        parts,
        part_in,
        others,
        others_in,
        weight_in,
        other_in,
        parted,
        parted_in,
        whole,
        whole_others,
        local_sem,
        load_sem,
        send_sem,
        recv_sem,
    ) = refs[30:]
    cov = hbm[0]
    (
        weight,
        scale,
        z_lane,
        z_supplier,
        z_region,
        z_company,
        group_owner,
        group_local,
        group_len,
        event_bin,
        observed,
        lane_supplier,
        supplier_region,
        region_company,
    ) = held_in
    dp = lax.axis_index("dp")
    mp = lax.axis_index("mp")
    z = lax.div(dp, 8)
    yc = lax.rem(dp, 8)
    right = lax.rem(mp + 1, 4)
    left = lax.rem(mp + 3, 4)

    def at_z(step):
        return {"dp": lax.rem(z + step, 16) * 8 + yc, "mp": mp}

    def at_yc(step):
        return {"dp": z * 8 + lax.rem(yc + step, 8), "mp": mp}

    def at_x(index):
        return {"dp": dp, "mp": index}

    loads = []
    for k in range(14):
        copy = pltpu.make_async_copy(hbm[k + 1], held_in[k], load_sem.at[k])
        copy.start()
        loads.append(copy)

    barrier = pltpu.get_barrier_semaphore()
    partners = [at_z(step) for step in STEPS]
    partners += [at_yc(step) for step in range(1, 8)]
    partners += [at_x(right), at_x(left)]
    for device in partners:
        pl.semaphore_signal(
            barrier, inc=1, device_id=device, device_id_type=pl.DeviceIdType.MESH
        )

    own_copies = []
    for c in range(CHUNKS):
        rows = pl.ds(c * CH, CH)
        copy = pltpu.make_async_copy(cov.at[rows], covers.at[mp, rows], local_sem.at[c])
        copy.start()
        own_copies.append(copy)

    count = [0]
    started = []

    def send(src, dst, device):
        slot = count[0]
        count[0] = slot + 1
        copy = pltpu.make_async_remote_copy(
            src_ref=src,
            dst_ref=dst,
            send_sem=send_sem.at[slot],
            recv_sem=recv_sem.at[slot],
            device_id=device,
            device_id_type=pl.DeviceIdType.MESH,
        )
        copy.start()
        started.append(copy)
        return copy

    def arrive(copies):
        for copy in copies:
            copy.wait_recv()

    def along_z(buf):
        return [send(buf.at[z], buf.at[z], at_z(step)) for step in STEPS]

    def plane(buf):
        return [send(buf.at[yc], buf.at[yc], at_yc(step)) for step in range(1, 8)]

    def scatter(source, target):
        return [
            send(source.at[lax.rem(yc + step, 8)], target.at[yc], at_yc(step))
            for step in range(1, 8)
        ]

    direct = {}
    passed = {}

    def launch(c):
        rows = pl.ds(c * CH, CH)
        block = covers.at[mp, rows]
        direct[c] = [
            send(cov.at[rows], block, at_x(right)),
            send(cov.at[rows], block, at_x(left)),
        ]

    def forward(c):
        arrive(direct[c])
        first = covers.at[left, pl.ds(c * CH, HALF)]
        second = covers.at[right, pl.ds(c * CH + HALF, HALF)]
        passed[c] = [send(first, first, at_x(right)), send(second, second, at_x(left))]

    for copy in loads:
        copy.wait()
    own_owner = group_owner[...].astype(F)
    own_local = group_local[...].astype(F)
    nodes[z, 0:32, :] = fold(fixed(z_lane[...])).astype(S)
    nodes[z, 32:48, :] = fold(fixed(z_supplier[...])).astype(S)
    of_lane = lane_supplier[...]
    lane_ids[z] = side(of_lane >> 6, of_lane & 63).astype(F)
    group_ids[yc] = side(own_owner, own_local)
    pl.semaphore_wait(barrier, len(partners))

    lane_id_copies = along_z(lane_ids)
    group_id_copies = plane(group_ids)
    for c in range(CHUNKS):
        launch(c)
    node_copies = along_z(nodes)

    weight_rows = weight[...].astype(B)
    company_effect = scale[0:1, :] * z_company[...]
    companies = region_company[...]
    company_pick = pick(iota((64, 8), 1) == column(companies.astype(F)).astype(I))
    region_effect = scale[1:2, :] * z_region[...] + mm(
        company_pick, company_effect, precision=HIGHEST
    )
    lens = group_len[...].astype(F)
    spread = jnp.where(
        (iota((16, 64), 1) >> 2) == iota((16, 64), 0), lens, jnp.zeros_like(lens)
    )
    lanes_of = pick((iota((64, 128), 0) & 3) == (iota((64, 128), 1) >> 5), B)
    live_len = mm(spread.astype(B), lanes_of).astype(I)
    ends = jnp.where((iota((16, 128), 1) & 31) < live_len, event_bin[...], -1)
    flags = observed[...].astype(F)

    arrive(group_id_copies)
    ids = jnp.concatenate([group_ids[j] for j in range(8)], axis=0).astype(I)
    owners, locals_ = ids[:, 0:64], ids[:, 64:128]
    held = jnp.where((owners & 7) == yc, owners >> 3, -1)
    lane_key = jnp.where(held >= 0, held * 64 + locals_, -1)
    lane_columns = [
        column(lane_key[j : j + 1, :].astype(F)).astype(I) for j in range(8)
    ]

    def flat(rows):
        return jnp.concatenate([rows[j : j + 1, :] for j in range(8)], axis=1)

    owner_pick = pick(iota((16, 512), 0) == flat(held), B)
    local_pick = iota((64, 512), 0) == flat(locals_)
    forward(0)
    forward(1)
    forward(2)

    arrive(lane_id_copies)
    table = jnp.concatenate([lane_ids[k] for k in range(16)], axis=0).T.astype(B)
    of_owner = mm(table, owner_pick)
    of_owner = of_owner[0:64, :] * 64.0 + of_owner[64:128, :]
    found = jnp.sum(jnp.where(local_pick, of_owner, jnp.float32(0.0)), axis=0, keepdims=True)
    found = jnp.concatenate([found[:, j * 64 : j * 64 + 64] for j in range(8)], axis=0)
    found_ids[yc] = side(found, jnp.zeros((8, 64), F))
    found_copies = plane(found_ids)
    forward(3)
    forward(4)

    def digits(first, size):
        value = nodes[:, first : first + size, :].reshape(16 * size, 128).astype(I)
        high = (value + 64) >> 7
        low = value - (high << 7)
        return side(high.astype(F).astype(B), low.astype(F).astype(B))

    def chosen(row, upper, table):
        got = mm(pick(iota((64, table.shape[0]), 1) == row, B), table)
        got = got[:, 0:128] * 128.0 + got[:, 128:256]
        return jnp.where(upper, got[:, 64:128], got[:, 0:64])

    arrive(node_copies)
    lane_table = digits(0, 32)
    lane_parts = []
    for j in range(8):
        key = lane_columns[j]
        row = jnp.where(key >= 0, (key >> 6) * 32 + (key & 31), -1)
        lane_parts.append(chosen(row, (key & 32) > 0, lane_table))
    forward(5)

    arrive(found_copies)
    suppliers = found_ids[0]
    for j in range(1, 8):
        suppliers = suppliers + found_ids[j]
    suppliers = suppliers[:, 0:64]
    own_supplier = jnp.sum(
        jnp.where(iota((8, 64), 0) == yc, suppliers, jnp.float32(0.0)), axis=0, keepdims=True
    )
    row_ids[z] = side(own_supplier, own_owner * 64.0 + own_local)
    suppliers = suppliers.astype(I)
    sup_table = digits(32, 16)
    sup_key = jnp.where(((suppliers >> 5) & 7) == yc, suppliers, -1)
    for j in range(8):
        key = column(sup_key[j : j + 1, :].astype(F)).astype(I)
        row = jnp.where(key >= 0, (key >> 8) * 16 + (key & 15), -1)
        sup_part = chosen(row, (key & 16) > 0, sup_table)
        reply[j] = side(lane_parts[j], sup_part).astype(I).astype(S)
    replied[yc] = reply[yc]
    reply_copies = scatter(reply, replied)
    row_id_copies = along_z(row_ids)
    forward(6)

    own_sup_col = column(own_supplier).astype(I)
    sup_row = pick(iota((64, 32), 1) == (own_sup_col >> 7), B)
    region_table = mm(sup_row, supplier_region[...].astype(F).astype(B))
    group_region = jnp.sum(
        jnp.where(iota((64, 128), 1) == (own_sup_col & 127), region_table, jnp.float32(0.0)),
        axis=1,
        keepdims=True,
    )
    region_col = group_region.astype(I)
    region_row = row_of(group_region).astype(I)
    group_effect = mm(
        pick(iota((64, 64), 1) == region_col), region_effect, precision=HIGHEST
    )
    forward(7)

    def covered(first, last):
        return jnp.concatenate([covers[k, first * CH : last * CH, :] for k in range(4)], axis=1)

    def project(c):
        own_copies[c].wait()
        arrive(passed[c])
        linear[:, c * CH : (c + 1) * CH] = mm(weight_rows, covered(c, c + 1), 1, 1)

    for c in range(CHUNKS):
        project(c)

    arrive(reply_copies)
    got = replied[0].astype(I)
    for j in range(1, 8):
        got = got + replied[j].astype(I)
    got = got.astype(F) * (1.0 / UNIT)
    lane_latent, sup_latent = got[:, 0:64], got[:, 64:128]
    path = scale[2:3, :] * sup_latent + group_effect
    offset = (scale[3:4, :] * lane_latent + path).astype(B)
    offset = offset.astype(F).T.astype(B)

    bins = iota((64, 128), 0) + mp * 64

    def score_block(s):
        at = slice(s * 128, (s + 1) * 128)
        expand = pick(iota((64, 128), 0) == (iota((64, 128), 1) >> 5) + 4 * s, B)
        eta = linear[:, at] + mm(offset, expand)
        hazard = jax.nn.sigmoid(eta)
        end = ends[s : s + 1, :]
        score = jnp.where(
            bins < end,
            -hazard,
            jnp.where(bins == end, flags[s : s + 1, :] - hazard, jnp.float32(0.0)),
        )
        scores[:, at] = score.astype(B)

    product = None
    for first in range(0, CHUNKS, 2):
        for block in range(first * CH // 128, (first + 2) * CH // 128):
            score_block(block)
        part = mm(scores[:, first * CH : (first + 2) * CH], covered(first, first + 2))
        product = part if product is None else product + part
    for j in range(8):
        k, half = divmod(j, 2)
        parts[j] = product[half * 32 : half * 32 + 32, k * 128 : (k + 1) * 128]
    part_in[yc] = parts[yc]
    part_copies = scatter(parts, part_in)

    group_pick = pick(iota((64, 2048), 0) == (iota((64, 2048), 1) >> 5), B)
    group_sum = mm(group_pick, scores[...], 1, 1)
    sums[z] = fold(group_sum).astype(B)
    sum_copies = along_z(sums)

    by_region = fold(
        mm(pick(iota((64, 64), 0) == region_row), group_sum, precision=HIGHEST)
    )
    scale_part = side(
        jnp.sum(lane_latent * group_sum, axis=0, keepdims=True),
        jnp.sum(sup_latent * group_sum, axis=0, keepdims=True),
    )
    for j in range(4):
        others[j] = by_region[j * 8 : j * 8 + 8, :]
    others[4] = jnp.where(iota((8, 128), 0) == 0, scale_part, jnp.float32(0.0))
    for j in range(5, 8):
        others[j] = jnp.zeros((8, 128), F)
    others_in[yc] = others[yc]
    other_copies = scatter(others, others_in)

    arrive(row_id_copies)
    held_rows = jnp.concatenate([row_ids[k] for k in range(16)], axis=0).astype(I)

    def along(start):
        return jnp.concatenate(
            [held_rows[k : k + 1, start : start + 32] for k in range(16)], axis=1
        )

    sup_along = side(along(0), along(32)) - z * 256
    lane_along = side(along(64), along(96)) - z * 512
    lane_hit = pick(iota((512, 1024), 0) == lane_along, B)
    sup_hit = pick(iota((256, 1024), 0) == sup_along, B)

    def added(buf, many):
        total = buf[0].astype(F)
        for k in range(1, many):
            total = total + buf[k].astype(F)
        return total

    arrive(part_copies)
    weight_in[z] = added(part_in, 8).astype(B)
    weight_copies = along_z(weight_in)
    arrive(other_copies)
    other_in[z] = added(others_in, 8)
    other_copies = along_z(other_in)

    arrive(sum_copies)
    gathered = stack(sums[...].reshape(512, 128), 512)
    by_lane = mm(lane_hit, gathered)
    by_supplier = mm(sup_hit, gathered)
    for j in range(8):
        parted[j, 0:32, :] = fold(by_lane[j * 64 : j * 64 + 64, :])
        parted[j, 32:48, :] = fold(by_supplier[j * 32 : j * 32 + 32, :])
    parted_in[yc] = parted[yc]
    lane_copies = scatter(parted, parted_in)
    arrive(weight_copies)
    whole[yc] = added(weight_in, 16)
    whole_copies = plane(whole)
    arrive(other_copies)
    whole_others[yc] = added(other_in, 16)
    whole_other_copies = plane(whole_others)

    arrive(lane_copies)
    total = added(parted_in, 8)
    grad_lane = scale[3:4, :] * stack(total, 32) - z_lane[...]
    grad_supplier = scale[2:3, :] * stack(total[32:48, :], 16) - z_supplier[...]
    result[0:32, 640:768] = side(grad_supplier, jnp.zeros((32, 64), F))

    arrive(whole_copies)
    for j in range(8):
        k, half = divmod(j, 2)
        at = (slice(half * 32, half * 32 + 32), slice(k * 128, (k + 1) * 128))
        result[at] = whole[j] - weight[at]
    arrive(whole_other_copies)
    by_region = jnp.concatenate([whole_others[j] for j in range(4)], axis=0)
    region_total = stack(by_region, 32)
    scale_total = whole_others[4, 0:1, :]
    company_total = mm(
        pick(iota((8, 64), 0) == companies), region_total, precision=HIGHEST
    )
    grad_region = scale[1:2, :] * region_total - z_region[...]
    grad_company = scale[0:1, :] * company_total - z_company[...]
    result[:, 512:640] = side(grad_lane, grad_region)
    result[32:40, 640:768] = side(grad_company, jnp.zeros((8, 64), F))
    of_company = jnp.sum(z_company[...] * company_total, axis=0, keepdims=True)
    of_region = jnp.sum(z_region[...] * region_total, axis=0, keepdims=True)
    rank = iota((8, 64), 0)
    grad_scale = jnp.where(
        rank == 0,
        of_company,
        jnp.where(
            rank == 1,
            of_region,
            jnp.where(rank == 2, scale_total[:, 64:128], scale_total[:, 0:64]),
        ),
    )
    result[40:48, 640:768] = side(grad_scale, jnp.zeros((8, 64), F))
    result[48:64, 640:768] = jnp.zeros((16, 128), F)

    for copy in started:
        copy.wait_send()


def publish(
    result, grad_weight, grad_lane, grad_supplier, grad_region, grad_company, grad_scale
):
    grad_weight[...] = result[:, 0:512]
    pair = result[:, 512:640]
    grad_lane[...] = pair[:, 0:64]
    grad_region[...] = pair[:, 64:128]
    rest = result[:, 640:768]
    grad_supplier[...] = rest[0:32, 0:64]
    grad_company[...] = rest[32:40, 0:64]
    grad_scale[...] = rest[40:44, 0:64]


def per_device(
    covariates,
    weight,
    scale,
    z_lane,
    z_supplier,
    z_region,
    z_company,
    group_owner,
    group_local,
    group_len,
    event_bin,
    observed,
    lane_supplier,
    supplier_region,
    region_company,
):
    vmem = pl.BlockSpec(memory_space=pltpu.VMEM)
    hbm = pl.BlockSpec(memory_space=pltpu.HBM)
    operands = (
        covariates,
        weight.T,
        scale,
        z_lane,
        z_supplier,
        z_region,
        z_company,
        group_owner.reshape(1, 64),
        group_local.reshape(1, 64),
        group_len.reshape(1, 64),
        event_bin.reshape(16, 128),
        observed.reshape(16, 128),
        lane_supplier.reshape(1, 64),
        supplier_region.reshape(32, 128),
        region_company.reshape(1, 64),
    )
    shapes = ((64, 512), (64, 64), (32, 64), (64, 64), (8, 64), (4, 64))
    shapes = tuple(jax.ShapeDtypeStruct(shape, F) for shape in shapes)
    slots = 224
    result = pl.pallas_call(
        kernel,
        out_shape=pltpu.VMEM((64, 768), F),
        in_specs=[hbm] * 15,
        out_specs=vmem,
        scratch_shapes=[pltpu.VMEM(op.shape, op.dtype) for op in operands[1:]]
        + [
            pltpu.VMEM((4, ROWS, 128), B),
            pltpu.VMEM((64, ROWS), F),
            pltpu.VMEM((64, ROWS), B),
            pltpu.VMEM((16, 48, 128), S),
            pltpu.VMEM((16, 1, 128), F),
            pltpu.VMEM((8, 1, 128), F),
            pltpu.VMEM((8, 8, 128), F),
            pltpu.VMEM((16, 1, 128), F),
            pltpu.VMEM((8, 64, 128), S),
            pltpu.VMEM((8, 64, 128), S),
            pltpu.VMEM((16, 32, 128), B),
            pltpu.VMEM((8, 32, 128), F),
            pltpu.VMEM((8, 32, 128), F),
            pltpu.VMEM((8, 8, 128), F),
            pltpu.VMEM((8, 8, 128), F),
            pltpu.VMEM((16, 32, 128), B),
            pltpu.VMEM((16, 8, 128), F),
            pltpu.VMEM((8, 48, 128), F),
            pltpu.VMEM((8, 48, 128), F),
            pltpu.VMEM((8, 32, 128), F),
            pltpu.VMEM((8, 8, 128), F),
            pltpu.SemaphoreType.DMA((CHUNKS,)),
            pltpu.SemaphoreType.DMA((14,)),
            pltpu.SemaphoreType.DMA((slots,)),
            pltpu.SemaphoreType.DMA((slots,)),
        ],
        compiler_params=pltpu.CompilerParams(
            collective_id=0, has_side_effects=True, vmem_limit_bytes=VMEM_BYTES
        ),
        name="hazard_gradient",
    )(*operands)
    results = pl.pallas_call(
        publish,
        out_shape=shapes,
        in_specs=[vmem],
        out_specs=tuple(pl.BlockSpec(shape.shape, lambda: (0, 0)) for shape in shapes),
        name="publish",
    )(result)
    return (results[0].T,) + tuple(results[1:])


def solution(mesh):
    in_specs = (
        P("dp", "mp"),
        P(None, "mp"),
        P(None, "mp"),
        P("dp", "mp"),
        P("dp", "mp"),
        P(None, "mp"),
        P(None, "mp"),
        P("dp", None),
        P("dp"),
        P("dp"),
        P("dp"),
        P("dp"),
        P("dp"),
        P(),
        P(),
    )
    out_specs = (
        P(None, "mp"),
        P("dp", "mp"),
        P("dp", "mp"),
        P(None, "mp"),
        P(None, "mp"),
        P(None, "mp"),
    )
    return jax.shard_map(
        per_device, mesh=mesh, in_specs=in_specs, out_specs=out_specs, check_vma=False
    )
```

```python
import jax
import jax.numpy as jnp
from jax import lax
from jax.experimental import pallas as pl
from jax.experimental.pallas import tpu as pltpu
from jax.sharding import PartitionSpec as P

HIGHEST = lax.Precision.HIGHEST
F = jnp.float32
B = jnp.bfloat16
I = jnp.int32
S = jnp.int16
VMEM_BYTES = 60 * 1024 * 1024
CHUNKS = 8
ROWS = 2048
CH = ROWS // CHUNKS
HALF = CH // 2
STEPS = (8, 7, 9, 6, 10, 5, 11, 4, 12, 3, 13, 2, 14, 1, 15)
UNIT = 5461.0


def iota(shape, axis):
    return lax.broadcasted_iota(I, shape, axis)


def mm(a, b, ca=1, cb=0, precision=None):
    return lax.dot_general(
        a, b, (((ca,), (cb,)), ((), ())), preferred_element_type=F, precision=precision
    )


def pick(cond, dtype=F):
    return jnp.where(cond, jnp.float32(1.0), jnp.float32(0.0)).astype(dtype)


def column(row):
    n = row.shape[1]
    return jnp.sum(
        jnp.where(iota((n, n), 0) == iota((n, n), 1), row, jnp.zeros_like(row)),
        axis=1,
        keepdims=True,
    )


def row_of(col):
    n = col.shape[0]
    return jnp.sum(
        jnp.where(iota((n, n), 0) == iota((n, n), 1), col, jnp.zeros_like(col)),
        axis=0,
        keepdims=True,
    )


def side(a, b):
    return jnp.concatenate([a, b], axis=1)


def fixed(value):
    return jnp.floor(value * UNIT + 0.5).astype(I)


def stack(value, rows):
    return jnp.concatenate([value[:rows, 0:64], value[:rows, 64:128]], axis=0)


def fold(value):
    half = value.shape[0] // 2
    return side(value[:half, :], value[half:, :])


def kernel(*refs):
    hbm = refs[:15]
    result = refs[15]
    held_in = refs[16:30]
    (
        covers,
        linear,
        scores,
        nodes,
        lane_ids,
        group_ids,
        found_ids,
        row_ids,
        reply,
        replied,
        sup_reply,
        sup_replied,
        sums,
        parts,
        part_in,
        weight_in,
        scale_rows,
        scale_in,
        parted,
        parted_in,
        whole,
        local_sem,
        load_sem,
        send_sem,
        recv_sem,
    ) = refs[30:]
    cov = hbm[0]
    (
        weight,
        scale,
        z_lane,
        z_supplier,
        z_region,
        z_company,
        group_owner,
        group_local,
        group_len,
        event_bin,
        observed,
        lane_supplier,
        supplier_region,
        region_company,
    ) = held_in
    dp = lax.axis_index("dp")
    mp = lax.axis_index("mp")
    z = lax.div(dp, 8)
    yc = lax.rem(dp, 8)
    right = lax.rem(mp + 1, 4)
    left = lax.rem(mp + 3, 4)

    def at_z(step):
        return {"dp": lax.rem(z + step, 16) * 8 + yc, "mp": mp}

    def at_yc(step):
        return {"dp": z * 8 + lax.rem(yc + step, 8), "mp": mp}

    def at_x(index):
        return {"dp": dp, "mp": index}

    barrier = pltpu.get_barrier_semaphore()
    partners = [at_z(step) for step in STEPS]
    partners += [at_yc(step) for step in range(1, 8)]
    partners += [at_x(right), at_x(left)]
    for device in partners:
        pl.semaphore_signal(
            barrier, inc=1, device_id=device, device_id_type=pl.DeviceIdType.MESH
        )

    loads = []
    for k in range(14):
        copy = pltpu.make_async_copy(hbm[k + 1], held_in[k], load_sem.at[k])
        copy.start()
        loads.append(copy)

    own_copies = []
    for c in range(CHUNKS):
        rows = pl.ds(c * CH, CH)
        copy = pltpu.make_async_copy(cov.at[rows], covers.at[mp, rows], local_sem.at[c])
        copy.start()
        own_copies.append(copy)

    count = [0]
    started = []

    def send(src, dst, device):
        slot = count[0]
        count[0] = slot + 1
        copy = pltpu.make_async_remote_copy(
            src_ref=src,
            dst_ref=dst,
            send_sem=send_sem.at[slot],
            recv_sem=recv_sem.at[slot],
            device_id=device,
            device_id_type=pl.DeviceIdType.MESH,
        )
        copy.start()
        started.append(copy)
        return copy

    def arrive(copies):
        for copy in copies:
            copy.wait_recv()

    def along_z(buf):
        return [send(buf.at[z], buf.at[z], at_z(step)) for step in STEPS]

    def plane(buf):
        return [send(buf.at[yc], buf.at[yc], at_yc(step)) for step in range(1, 8)]

    def scatter(source, target):
        return [
            send(source.at[lax.rem(yc + step, 8)], target.at[yc], at_yc(step))
            for step in range(1, 8)
        ]

    direct = {}
    passed = {}

    def launch(c):
        rows = pl.ds(c * CH, CH)
        block = covers.at[mp, rows]
        direct[c] = [
            send(cov.at[rows], block, at_x(right)),
            send(cov.at[rows], block, at_x(left)),
        ]

    def forward(c):
        arrive(direct[c])
        first = covers.at[left, pl.ds(c * CH, HALF)]
        second = covers.at[right, pl.ds(c * CH + HALF, HALF)]
        passed[c] = [send(first, first, at_x(right)), send(second, second, at_x(left))]

    for copy in loads:
        copy.wait()
    own_owner = group_owner[...].astype(F)
    own_local = group_local[...].astype(F)
    nodes[z, 0:32, :] = fold(fixed(z_lane[...])).astype(S)
    nodes[z, 32:48, :] = fold(fixed(z_supplier[...])).astype(S)
    of_lane = lane_supplier[...]
    lane_ids[z] = side(of_lane >> 6, of_lane & 63).astype(F)
    group_ids[yc] = side(own_owner, own_local)
    pl.semaphore_wait(barrier, len(partners))

    for c in range(2):
        launch(c)
    lane_id_copies = along_z(lane_ids)
    group_id_copies = plane(group_ids)
    for c in range(2, 4):
        launch(c)
    node_copies = along_z(nodes)
    for c in range(4, CHUNKS):
        launch(c)

    weight_rows = weight[...].astype(B)
    company_effect = scale[0:1, :] * z_company[...]
    companies = region_company[...]
    company_pick = pick(iota((64, 8), 1) == column(companies.astype(F)).astype(I))
    region_effect = scale[1:2, :] * z_region[...] + mm(
        company_pick, company_effect, precision=HIGHEST
    )
    lens = group_len[...].astype(F)
    spread = jnp.where(
        (iota((16, 64), 1) >> 2) == iota((16, 64), 0), lens, jnp.zeros_like(lens)
    )
    lanes_of = pick((iota((64, 128), 0) & 3) == (iota((64, 128), 1) >> 5), B)
    live_len = mm(spread.astype(B), lanes_of).astype(I)
    ends = jnp.where((iota((16, 128), 1) & 31) < live_len, event_bin[...], -1)
    flags = observed[...].astype(F)

    arrive(group_id_copies)
    ids = jnp.concatenate([group_ids[j] for j in range(8)], axis=0).astype(I)
    owners, locals_ = ids[:, 0:64], ids[:, 64:128]
    held = jnp.where((owners & 7) == yc, owners >> 3, -1)
    lane_key = jnp.where(held >= 0, held * 64 + locals_, -1)
    lane_columns = [
        column(lane_key[j : j + 1, :].astype(F)).astype(I) for j in range(8)
    ]

    def flat(rows):
        return jnp.concatenate([rows[j : j + 1, :] for j in range(8)], axis=1)

    owner_pick = pick(iota((16, 512), 0) == flat(held), B)
    local_pick = iota((64, 512), 0) == flat(locals_)
    forward(0)
    forward(1)
    forward(2)

    arrive(lane_id_copies)
    table = jnp.concatenate([lane_ids[k] for k in range(16)], axis=0).T.astype(B)
    of_owner = mm(table, owner_pick)
    of_owner = of_owner[0:64, :] * 64.0 + of_owner[64:128, :]
    found = jnp.sum(jnp.where(local_pick, of_owner, jnp.float32(0.0)), axis=0, keepdims=True)
    found = jnp.concatenate([found[:, j * 64 : j * 64 + 64] for j in range(8)], axis=0)
    found_ids[yc] = side(found, jnp.zeros((8, 64), F))
    found_copies = plane(found_ids)
    forward(3)
    forward(4)

    def digits(first, size):
        value = nodes[:, first : first + size, :].reshape(16 * size, 128).astype(I)
        high = (value + 64) >> 7
        low = value - (high << 7)
        return side(high.astype(F).astype(B), low.astype(F).astype(B))

    def chosen(row, upper, table):
        got = mm(pick(iota((64, table.shape[0]), 1) == row, B), table)
        got = got[:, 0:128] * 128.0 + got[:, 128:256]
        return jnp.where(upper, got[:, 64:128], got[:, 0:64])

    arrive(node_copies)
    lane_table = digits(0, 32)
    for j in range(8):
        key = lane_columns[j]
        row = jnp.where(key >= 0, (key >> 6) * 32 + (key & 31), -1)
        reply[j] = fold(chosen(row, (key & 32) > 0, lane_table)).astype(I).astype(S)
    replied[yc] = reply[yc]
    reply_copies = scatter(reply, replied)
    forward(5)

    arrive(found_copies)
    suppliers = found_ids[0]
    for j in range(1, 8):
        suppliers = suppliers + found_ids[j]
    suppliers = suppliers[:, 0:64]
    own_supplier = jnp.sum(
        jnp.where(iota((8, 64), 0) == yc, suppliers, jnp.float32(0.0)), axis=0, keepdims=True
    )
    suppliers = suppliers.astype(I)
    sup_table = digits(32, 16)
    sup_key = jnp.where(((suppliers >> 5) & 7) == yc, suppliers, -1)
    for j in range(8):
        key = column(sup_key[j : j + 1, :].astype(F)).astype(I)
        row = jnp.where(key >= 0, (key >> 8) * 16 + (key & 15), -1)
        sup_reply[j] = fold(chosen(row, (key & 16) > 0, sup_table)).astype(I).astype(S)
    sup_replied[yc] = sup_reply[yc]
    reply_copies += scatter(sup_reply, sup_replied)
    forward(6)

    own_sup_col = column(own_supplier).astype(I)
    sup_row = pick(iota((64, 32), 1) == (own_sup_col >> 7), B)
    region_table = mm(sup_row, supplier_region[...].astype(F).astype(B))
    group_region = jnp.sum(
        jnp.where(iota((64, 128), 1) == (own_sup_col & 127), region_table, jnp.float32(0.0)),
        axis=1,
        keepdims=True,
    )
    region_col = group_region.astype(I)
    row_ids[z] = side(
        own_supplier * 64.0 + row_of(group_region), own_owner * 64.0 + own_local
    )
    row_id_copies = along_z(row_ids)
    group_effect = mm(
        pick(iota((64, 64), 1) == region_col), region_effect, precision=HIGHEST
    )
    forward(7)

    def covered(first, last):
        return jnp.concatenate([covers[k, first * CH : last * CH, :] for k in range(4)], axis=1)

    def project(c):
        own_copies[c].wait()
        arrive(passed[c])
        linear[:, c * CH : (c + 1) * CH] = mm(weight_rows, covered(c, c + 1), 1, 1)

    for c in range(CHUNKS):
        project(c)

    arrive(reply_copies)

    def latent(buf):
        got = buf[0].astype(I)
        for j in range(1, 8):
            got = got + buf[j].astype(I)
        return stack(got.astype(F) * (1.0 / UNIT), 32)

    lane_latent, sup_latent = latent(replied), latent(sup_replied)
    path = scale[2:3, :] * sup_latent + group_effect
    offset = (scale[3:4, :] * lane_latent + path).astype(B)
    offset = offset.astype(F).T.astype(B)

    bins = iota((64, 128), 0) + mp * 64

    def score_block(s):
        at = slice(s * 128, (s + 1) * 128)
        expand = pick(iota((64, 128), 0) == (iota((64, 128), 1) >> 5) + 4 * s, B)
        eta = linear[:, at] + mm(offset, expand)
        hazard = jax.nn.sigmoid(eta)
        end = ends[s : s + 1, :]
        score = jnp.where(
            bins < end,
            -hazard,
            jnp.where(bins == end, flags[s : s + 1, :] - hazard, jnp.float32(0.0)),
        )
        scores[:, at] = score.astype(B)

    product = None
    for first in range(0, CHUNKS, 2):
        for block in range(first * CH // 128, (first + 2) * CH // 128):
            score_block(block)
        part = mm(scores[:, first * CH : (first + 2) * CH], covered(first, first + 2))
        product = part if product is None else product + part
    for j in range(8):
        k, half = divmod(j, 2)
        block = product[half * 32 : half * 32 + 32, k * 128 : (k + 1) * 128]
        parts[j] = block.astype(B)
    part_in[yc] = parts[yc]
    part_copies = scatter(parts, part_in)

    group_pick = pick(iota((64, 2048), 0) == (iota((64, 2048), 1) >> 5), B)
    group_sum = mm(group_pick, scores[...], 1, 1)
    sums[z] = fold(group_sum).astype(B)
    sum_copies = along_z(sums)

    scale_rows[z] = side(
        jnp.sum(lane_latent * group_sum, axis=0, keepdims=True),
        jnp.sum(sup_latent * group_sum, axis=0, keepdims=True),
    )
    scale_copies = along_z(scale_rows)

    arrive(row_id_copies)
    held_rows = jnp.concatenate([row_ids[k] for k in range(16)], axis=0).astype(I)

    def along(start):
        return jnp.concatenate(
            [held_rows[k : k + 1, start : start + 32] for k in range(16)], axis=1
        )

    sup_along = side(along(0), along(32))
    region_along = sup_along & 63
    sup_along = (sup_along >> 6) - z * 256
    lane_along = side(along(64), along(96)) - z * 512
    lane_hit = pick(iota((512, 1024), 0) == lane_along, B)
    sup_hit = pick(iota((256, 1024), 0) == sup_along, B)
    region_hit = pick(iota((64, 1024), 0) == region_along, B)

    def added(buf, many):
        total = buf[0].astype(F)
        for k in range(1, many):
            total = total + buf[k].astype(F)
        return total

    arrive(part_copies)
    weight_in[z] = added(part_in, 8).astype(B)
    weight_copies = along_z(weight_in)

    arrive(sum_copies)
    gathered = stack(sums[...].reshape(512, 128), 512)
    by_lane = mm(lane_hit, gathered)
    by_supplier = mm(sup_hit, gathered)
    by_region = fold(mm(region_hit, gathered)).astype(B)
    for j in range(8):
        parted[j, 0:32, :] = fold(by_lane[j * 64 : j * 64 + 64, :]).astype(B)
        parted[j, 32:48, :] = fold(by_supplier[j * 32 : j * 32 + 32, :]).astype(B)
        parted[j, 48:80, :] = by_region
    parted_in[yc] = parted[yc]
    lane_copies = scatter(parted, parted_in)
    arrive(scale_copies)
    scale_in[yc] = added(scale_rows, 16)
    scale_copies = plane(scale_in)

    arrive(weight_copies)
    whole[yc] = added(weight_in, 16)
    whole_copies = plane(whole)

    arrive(lane_copies)
    total = added(parted_in, 8)
    grad_lane = scale[3:4, :] * stack(total, 32) - z_lane[...]
    grad_supplier = scale[2:3, :] * stack(total[32:48, :], 16) - z_supplier[...]
    region_total = stack(total[48:80, :], 32)
    result[0:32, 640:768] = side(grad_supplier, jnp.zeros((32, 64), F))
    arrive(scale_copies)
    scale_total = added(scale_in, 8)
    company_total = mm(
        pick(iota((8, 64), 0) == companies), region_total, precision=HIGHEST
    )
    grad_region = scale[1:2, :] * region_total - z_region[...]
    grad_company = scale[0:1, :] * company_total - z_company[...]
    result[:, 512:640] = side(grad_lane, grad_region)
    result[32:40, 640:768] = side(grad_company, jnp.zeros((8, 64), F))
    of_company = jnp.sum(z_company[...] * company_total, axis=0, keepdims=True)
    of_region = jnp.sum(z_region[...] * region_total, axis=0, keepdims=True)
    rank = iota((8, 64), 0)
    grad_scale = jnp.where(
        rank == 0,
        of_company,
        jnp.where(
            rank == 1,
            of_region,
            jnp.where(rank == 2, scale_total[:, 64:128], scale_total[:, 0:64]),
        ),
    )
    result[40:48, 640:768] = side(grad_scale, jnp.zeros((8, 64), F))
    result[48:64, 640:768] = jnp.zeros((16, 128), F)

    arrive(whole_copies)
    for j in range(8):
        k, half = divmod(j, 2)
        at = (slice(half * 32, half * 32 + 32), slice(k * 128, (k + 1) * 128))
        result[at] = whole[j] - weight[at]

    for copy in started:
        copy.wait_send()


def publish(
    result, grad_weight, grad_lane, grad_supplier, grad_region, grad_company, grad_scale
):
    grad_weight[...] = result[:, 0:512]
    pair = result[:, 512:640]
    grad_lane[...] = pair[:, 0:64]
    grad_region[...] = pair[:, 64:128]
    rest = result[:, 640:768]
    grad_supplier[...] = rest[0:32, 0:64]
    grad_company[...] = rest[32:40, 0:64]
    grad_scale[...] = rest[40:44, 0:64]


def per_device(
    covariates,
    weight,
    scale,
    z_lane,
    z_supplier,
    z_region,
    z_company,
    group_owner,
    group_local,
    group_len,
    event_bin,
    observed,
    lane_supplier,
    supplier_region,
    region_company,
):
    vmem = pl.BlockSpec(memory_space=pltpu.VMEM)
    hbm = pl.BlockSpec(memory_space=pltpu.HBM)
    operands = (
        covariates,
        weight.T,
        scale,
        z_lane,
        z_supplier,
        z_region,
        z_company,
        group_owner.reshape(1, 64),
        group_local.reshape(1, 64),
        group_len.reshape(1, 64),
        event_bin.reshape(16, 128),
        observed.reshape(16, 128),
        lane_supplier.reshape(1, 64),
        supplier_region.reshape(32, 128),
        region_company.reshape(1, 64),
    )
    shapes = ((64, 512), (64, 64), (32, 64), (64, 64), (8, 64), (4, 64))
    shapes = tuple(jax.ShapeDtypeStruct(shape, F) for shape in shapes)
    slots = 224
    result = pl.pallas_call(
        kernel,
        out_shape=pltpu.VMEM((64, 768), F),
        in_specs=[hbm] * 15,
        out_specs=vmem,
        scratch_shapes=[pltpu.VMEM(op.shape, op.dtype) for op in operands[1:]]
        + [
            pltpu.VMEM((4, ROWS, 128), B),
            pltpu.VMEM((64, ROWS), F),
            pltpu.VMEM((64, ROWS), B),
            pltpu.VMEM((16, 48, 128), S),
            pltpu.VMEM((16, 1, 128), F),
            pltpu.VMEM((8, 1, 128), F),
            pltpu.VMEM((8, 8, 128), F),
            pltpu.VMEM((16, 1, 128), F),
            pltpu.VMEM((8, 32, 128), S),
            pltpu.VMEM((8, 32, 128), S),
            pltpu.VMEM((8, 32, 128), S),
            pltpu.VMEM((8, 32, 128), S),
            pltpu.VMEM((16, 32, 128), B),
            pltpu.VMEM((8, 32, 128), B),
            pltpu.VMEM((8, 32, 128), B),
            pltpu.VMEM((16, 32, 128), B),
            pltpu.VMEM((16, 1, 128), F),
            pltpu.VMEM((8, 1, 128), F),
            pltpu.VMEM((8, 80, 128), B),
            pltpu.VMEM((8, 80, 128), B),
            pltpu.VMEM((8, 32, 128), F),
            pltpu.SemaphoreType.DMA((CHUNKS,)),
            pltpu.SemaphoreType.DMA((14,)),
            pltpu.SemaphoreType.DMA((slots,)),
            pltpu.SemaphoreType.DMA((slots,)),
        ],
        compiler_params=pltpu.CompilerParams(
            collective_id=0, has_side_effects=True, vmem_limit_bytes=VMEM_BYTES
        ),
        name="hazard_gradient",
    )(*operands)
    results = pl.pallas_call(
        publish,
        out_shape=shapes,
        in_specs=[vmem],
        out_specs=tuple(pl.BlockSpec(shape.shape, lambda: (0, 0)) for shape in shapes),
        name="publish",
    )(result)
    return (results[0].T,) + tuple(results[1:])


def solution(mesh):
    in_specs = (
        P("dp", "mp"),
        P(None, "mp"),
        P(None, "mp"),
        P("dp", "mp"),
        P("dp", "mp"),
        P(None, "mp"),
        P(None, "mp"),
        P("dp", None),
        P("dp"),
        P("dp"),
        P("dp"),
        P("dp"),
        P("dp"),
        P(),
        P(),
    )
    out_specs = (
        P(None, "mp"),
        P("dp", "mp"),
        P("dp", "mp"),
        P(None, "mp"),
        P(None, "mp"),
        P(None, "mp"),
    )
    return jax.shard_map(
        per_device, mesh=mesh, in_specs=in_specs, out_specs=out_specs, check_vma=False
    )
```

```python
import jax
import jax.numpy as jnp
from jax import lax
from jax.experimental import pallas as pl
from jax.experimental.pallas import tpu as pltpu
from jax.sharding import PartitionSpec as P

HIGHEST = lax.Precision.HIGHEST
F = jnp.float32
B = jnp.bfloat16
I = jnp.int32
S = jnp.int16
VMEM_BYTES = 60 * 1024 * 1024
CHUNKS = 8
ROWS = 2048
CH = ROWS // CHUNKS
HALF = CH // 2
STEPS = (8, 7, 9, 6, 10, 5, 11, 4, 12, 3, 13, 2, 14, 1, 15)
UNIT = 5461.0


def iota(shape, axis):
    return lax.broadcasted_iota(I, shape, axis)


def mm(a, b, ca=1, cb=0, precision=None):
    return lax.dot_general(
        a, b, (((ca,), (cb,)), ((), ())), preferred_element_type=F, precision=precision
    )


def pick(cond, dtype=F):
    return jnp.where(cond, jnp.float32(1.0), jnp.float32(0.0)).astype(dtype)


def column(row):
    n = row.shape[1]
    return jnp.sum(
        jnp.where(iota((n, n), 0) == iota((n, n), 1), row, jnp.zeros_like(row)),
        axis=1,
        keepdims=True,
    )


def row_of(col):
    n = col.shape[0]
    return jnp.sum(
        jnp.where(iota((n, n), 0) == iota((n, n), 1), col, jnp.zeros_like(col)),
        axis=0,
        keepdims=True,
    )


def side(a, b):
    return jnp.concatenate([a, b], axis=1)


def fixed(value):
    return jnp.floor(value * UNIT + 0.5).astype(I)


def stack(value, rows):
    return jnp.concatenate([value[:rows, 0:64], value[:rows, 64:128]], axis=0)


def fold(value):
    half = value.shape[0] // 2
    return side(value[:half, :], value[half:, :])


def kernel(*refs):
    hbm = refs[:15]
    result = refs[15]
    held_in = refs[16:30]
    (
        covers,
        linear,
        scores,
        nodes,
        lane_ids,
        group_ids,
        found_ids,
        row_ids,
        reply,
        replied,
        sup_reply,
        sup_replied,
        sums,
        parts,
        part_in,
        weight_in,
        scale_rows,
        scale_in,
        parted,
        parted_in,
        whole,
        local_sem,
        load_sem,
        send_sem,
        recv_sem,
    ) = refs[30:]
    cov = hbm[0]
    (
        weight,
        scale,
        z_lane,
        z_supplier,
        z_region,
        z_company,
        group_owner,
        group_local,
        group_len,
        event_bin,
        observed,
        lane_supplier,
        supplier_region,
        region_company,
    ) = held_in
    dp = lax.axis_index("dp")
    mp = lax.axis_index("mp")
    z = lax.div(dp, 8)
    yc = lax.rem(dp, 8)
    right = lax.rem(mp + 1, 4)
    left = lax.rem(mp + 3, 4)

    def at_z(step):
        return {"dp": lax.rem(z + step, 16) * 8 + yc, "mp": mp}

    def at_yc(step):
        return {"dp": z * 8 + lax.rem(yc + step, 8), "mp": mp}

    def at_x(index):
        return {"dp": dp, "mp": index}

    barrier = pltpu.get_barrier_semaphore()
    partners = [at_z(step) for step in STEPS]
    partners += [at_yc(step) for step in range(1, 8)]
    partners += [at_x(right), at_x(left)]
    for device in partners:
        pl.semaphore_signal(
            barrier, inc=1, device_id=device, device_id_type=pl.DeviceIdType.MESH
        )

    loads = []
    for k in range(14):
        copy = pltpu.make_async_copy(hbm[k + 1], held_in[k], load_sem.at[k])
        copy.start()
        loads.append(copy)

    own_copies = []
    for c in range(CHUNKS):
        rows = pl.ds(c * CH, CH)
        copy = pltpu.make_async_copy(cov.at[rows], covers.at[mp, rows], local_sem.at[c])
        copy.start()
        own_copies.append(copy)

    count = [0]
    started = []

    def send(src, dst, device):
        slot = count[0]
        count[0] = slot + 1
        copy = pltpu.make_async_remote_copy(
            src_ref=src,
            dst_ref=dst,
            send_sem=send_sem.at[slot],
            recv_sem=recv_sem.at[slot],
            device_id=device,
            device_id_type=pl.DeviceIdType.MESH,
        )
        copy.start()
        started.append(copy)
        return copy

    def settle(first, last):
        for copy in started[first:last]:
            copy.wait_send()

    def arrive(copies):
        for copy in copies:
            copy.wait_recv()

    def along_z(buf):
        return [send(buf.at[z], buf.at[z], at_z(step)) for step in STEPS]

    def plane(buf):
        return [send(buf.at[yc], buf.at[yc], at_yc(step)) for step in range(1, 8)]

    def scatter(source, target):
        return [
            send(source.at[lax.rem(yc + step, 8)], target.at[yc], at_yc(step))
            for step in range(1, 8)
        ]

    direct = {}
    passed = {}

    def launch(c):
        rows = pl.ds(c * CH, CH)
        block = covers.at[mp, rows]
        direct[c] = [
            send(cov.at[rows], block, at_x(right)),
            send(cov.at[rows], block, at_x(left)),
        ]

    def forward(c):
        arrive(direct[c])
        first = covers.at[left, pl.ds(c * CH, HALF)]
        second = covers.at[right, pl.ds(c * CH + HALF, HALF)]
        passed[c] = [send(first, first, at_x(right)), send(second, second, at_x(left))]

    for copy in loads:
        copy.wait()
    own_owner = group_owner[...].astype(F)
    own_local = group_local[...].astype(F)
    nodes[z, 0:32, :] = fold(fixed(z_lane[...])).astype(S)
    nodes[z, 32:48, :] = fold(fixed(z_supplier[...])).astype(S)
    of_lane = lane_supplier[...]
    lane_ids[z] = side(of_lane >> 6, of_lane & 63).astype(F)
    group_ids[yc] = side(own_owner, own_local)
    pl.semaphore_wait(barrier, len(partners))

    for c in range(2):
        launch(c)
    lane_id_copies = along_z(lane_ids)
    group_id_copies = plane(group_ids)
    for c in range(2, 4):
        launch(c)
    node_copies = along_z(nodes)
    for c in range(4, CHUNKS):
        launch(c)

    weight_rows = weight[...].astype(B)
    company_effect = scale[0:1, :] * z_company[...]
    companies = region_company[...]
    company_pick = pick(iota((64, 8), 1) == column(companies.astype(F)).astype(I))
    region_effect = scale[1:2, :] * z_region[...] + mm(
        company_pick, company_effect, precision=HIGHEST
    )
    lens = group_len[...].astype(F)
    spread = jnp.where(
        (iota((16, 64), 1) >> 2) == iota((16, 64), 0), lens, jnp.zeros_like(lens)
    )
    lanes_of = pick((iota((64, 128), 0) & 3) == (iota((64, 128), 1) >> 5), B)
    live_len = mm(spread.astype(B), lanes_of).astype(I)
    ends = jnp.where((iota((16, 128), 1) & 31) < live_len, event_bin[...], -1)
    flags = observed[...].astype(F)

    arrive(group_id_copies)
    ids = jnp.concatenate([group_ids[j] for j in range(8)], axis=0).astype(I)
    owners, locals_ = ids[:, 0:64], ids[:, 64:128]
    held = jnp.where((owners & 7) == yc, owners >> 3, -1)
    lane_key = jnp.where(held >= 0, held * 64 + locals_, -1)
    lane_columns = [
        column(lane_key[j : j + 1, :].astype(F)).astype(I) for j in range(8)
    ]

    def flat(rows):
        return jnp.concatenate([rows[j : j + 1, :] for j in range(8)], axis=1)

    owner_pick = pick(iota((16, 512), 0) == flat(held), B)
    local_pick = iota((64, 512), 0) == flat(locals_)
    forward(0)
    forward(1)
    forward(2)

    arrive(lane_id_copies)
    table = jnp.concatenate([lane_ids[k] for k in range(16)], axis=0).T.astype(B)
    of_owner = mm(table, owner_pick)
    of_owner = of_owner[0:64, :] * 64.0 + of_owner[64:128, :]
    found = jnp.sum(jnp.where(local_pick, of_owner, jnp.float32(0.0)), axis=0, keepdims=True)
    found = jnp.concatenate([found[:, j * 64 : j * 64 + 64] for j in range(8)], axis=0)
    found_ids[yc] = side(found, jnp.zeros((8, 64), F))
    found_copies = plane(found_ids)
    forward(3)
    forward(4)

    def digits(first, size):
        value = nodes[:, first : first + size, :].reshape(16 * size, 128).astype(I)
        high = (value + 64) >> 7
        low = value - (high << 7)
        return side(high.astype(F).astype(B), low.astype(F).astype(B))

    def chosen(row, upper, table):
        got = mm(pick(iota((64, table.shape[0]), 1) == row, B), table)
        got = got[:, 0:128] * 128.0 + got[:, 128:256]
        return jnp.where(upper, got[:, 64:128], got[:, 0:64])

    arrive(node_copies)
    lane_table = digits(0, 32)
    for j in range(8):
        key = lane_columns[j]
        row = jnp.where(key >= 0, (key >> 6) * 32 + (key & 31), -1)
        reply[j] = fold(chosen(row, (key & 32) > 0, lane_table)).astype(I).astype(S)
    replied[yc] = reply[yc]
    reply_copies = scatter(reply, replied)
    forward(5)

    arrive(found_copies)
    suppliers = found_ids[0]
    for j in range(1, 8):
        suppliers = suppliers + found_ids[j]
    suppliers = suppliers[:, 0:64]
    own_supplier = jnp.sum(
        jnp.where(iota((8, 64), 0) == yc, suppliers, jnp.float32(0.0)), axis=0, keepdims=True
    )
    suppliers = suppliers.astype(I)
    sup_table = digits(32, 16)
    sup_key = jnp.where(((suppliers >> 5) & 7) == yc, suppliers, -1)
    for j in range(8):
        key = column(sup_key[j : j + 1, :].astype(F)).astype(I)
        row = jnp.where(key >= 0, (key >> 8) * 16 + (key & 15), -1)
        sup_reply[j] = fold(chosen(row, (key & 16) > 0, sup_table)).astype(I).astype(S)
    sup_replied[yc] = sup_reply[yc]
    reply_copies += scatter(sup_reply, sup_replied)
    forward(6)

    own_sup_col = column(own_supplier).astype(I)
    sup_row = pick(iota((64, 32), 1) == (own_sup_col >> 7), B)
    region_table = mm(sup_row, supplier_region[...].astype(F).astype(B))
    group_region = jnp.sum(
        jnp.where(iota((64, 128), 1) == (own_sup_col & 127), region_table, jnp.float32(0.0)),
        axis=1,
        keepdims=True,
    )
    region_col = group_region.astype(I)
    row_ids[z] = side(
        own_supplier * 64.0 + row_of(group_region), own_owner * 64.0 + own_local
    )
    row_id_copies = along_z(row_ids)
    group_effect = mm(
        pick(iota((64, 64), 1) == region_col), region_effect, precision=HIGHEST
    )
    forward(7)

    def covered(first, last):
        return jnp.concatenate([covers[k, first * CH : last * CH, :] for k in range(4)], axis=1)

    def project(c):
        own_copies[c].wait()
        arrive(passed[c])
        linear[:, c * CH : (c + 1) * CH] = mm(weight_rows, covered(c, c + 1), 1, 1)

    for c in range(CHUNKS):
        project(c)

    arrive(reply_copies)

    def latent(buf):
        got = buf[0].astype(I)
        for j in range(1, 8):
            got = got + buf[j].astype(I)
        return stack(got.astype(F) * (1.0 / UNIT), 32)

    lane_latent, sup_latent = latent(replied), latent(sup_replied)
    path = scale[2:3, :] * sup_latent + group_effect
    offset = (scale[3:4, :] * lane_latent + path).astype(B)
    offset = offset.astype(F).T.astype(B)

    bins = iota((64, 128), 0) + mp * 64

    def score_block(s):
        at = slice(s * 128, (s + 1) * 128)
        expand = pick(iota((64, 128), 0) == (iota((64, 128), 1) >> 5) + 4 * s, B)
        eta = linear[:, at] + mm(offset, expand)
        hazard = jax.nn.sigmoid(eta)
        end = ends[s : s + 1, :]
        score = jnp.where(
            bins < end,
            -hazard,
            jnp.where(bins == end, flags[s : s + 1, :] - hazard, jnp.float32(0.0)),
        )
        scores[:, at] = score.astype(B)

    for block in range(16):
        score_block(block)
    group_pick = pick(iota((64, 2048), 0) == (iota((64, 2048), 1) >> 5), B)
    group_sum = mm(group_pick, scores[...], 1, 1)
    sums[z] = fold(group_sum).astype(B)
    sum_copies = along_z(sums)

    product = None
    for first in range(0, CHUNKS, 2):
        part = mm(scores[:, first * CH : (first + 2) * CH], covered(first, first + 2))
        product = part if product is None else product + part
    for j in range(8):
        k, half = divmod(j, 2)
        block = product[half * 32 : half * 32 + 32, k * 128 : (k + 1) * 128]
        parts[j] = block.astype(B)
    part_in[yc] = parts[yc]
    before_parts = count[0]
    part_copies = scatter(parts, part_in)

    scale_rows[z] = side(
        jnp.sum(lane_latent * group_sum, axis=0, keepdims=True),
        jnp.sum(sup_latent * group_sum, axis=0, keepdims=True),
    )
    scale_copies = along_z(scale_rows)

    arrive(row_id_copies)
    held_rows = jnp.concatenate([row_ids[k] for k in range(16)], axis=0).astype(I)

    def along(start):
        return jnp.concatenate(
            [held_rows[k : k + 1, start : start + 32] for k in range(16)], axis=1
        )

    sup_along = side(along(0), along(32))
    region_along = sup_along & 63
    sup_along = (sup_along >> 6) - z * 256
    lane_along = side(along(64), along(96)) - z * 512
    lane_hit = pick(iota((512, 1024), 0) == lane_along, B)
    sup_hit = pick(iota((256, 1024), 0) == sup_along, B)
    region_hit = pick(iota((64, 1024), 0) == region_along, B)

    def added(buf, many):
        total = buf[0].astype(F)
        for k in range(1, many):
            total = total + buf[k].astype(F)
        return total

    arrive(part_copies)
    weight_in[z] = added(part_in, 8).astype(B)
    weight_copies = along_z(weight_in)

    arrive(sum_copies)
    gathered = stack(sums[...].reshape(512, 128), 512)
    by_lane = mm(lane_hit, gathered)
    by_supplier = mm(sup_hit, gathered)
    by_region = fold(mm(region_hit, gathered)).astype(B)
    for j in range(8):
        parted[j, 0:32, :] = fold(by_lane[j * 64 : j * 64 + 64, :]).astype(B)
        parted[j, 32:48, :] = fold(by_supplier[j * 32 : j * 32 + 32, :]).astype(B)
        parted[j, 48:80, :] = by_region
    parted_in[yc] = parted[yc]
    lane_copies = scatter(parted, parted_in)
    arrive(scale_copies)
    scale_in[yc] = added(scale_rows, 16)
    scale_copies = plane(scale_in)

    settle(0, before_parts)
    arrive(weight_copies)
    whole[yc] = added(weight_in, 16)
    before_whole = count[0]
    whole_copies = plane(whole)

    arrive(lane_copies)
    total = added(parted_in, 8)
    grad_lane = scale[3:4, :] * stack(total, 32) - z_lane[...]
    grad_supplier = scale[2:3, :] * stack(total[32:48, :], 16) - z_supplier[...]
    region_total = stack(total[48:80, :], 32)
    result[0:32, 640:768] = side(grad_supplier, jnp.zeros((32, 64), F))
    arrive(scale_copies)
    scale_total = added(scale_in, 8)
    company_total = mm(
        pick(iota((8, 64), 0) == companies), region_total, precision=HIGHEST
    )
    grad_region = scale[1:2, :] * region_total - z_region[...]
    grad_company = scale[0:1, :] * company_total - z_company[...]
    result[:, 512:640] = side(grad_lane, grad_region)
    result[32:40, 640:768] = side(grad_company, jnp.zeros((8, 64), F))
    of_company = jnp.sum(z_company[...] * company_total, axis=0, keepdims=True)
    of_region = jnp.sum(z_region[...] * region_total, axis=0, keepdims=True)
    rank = iota((8, 64), 0)
    grad_scale = jnp.where(
        rank == 0,
        of_company,
        jnp.where(
            rank == 1,
            of_region,
            jnp.where(rank == 2, scale_total[:, 64:128], scale_total[:, 0:64]),
        ),
    )
    result[40:48, 640:768] = side(grad_scale, jnp.zeros((8, 64), F))
    result[48:64, 640:768] = jnp.zeros((16, 128), F)

    settle(before_parts, before_whole)
    arrive(whole_copies)
    for j in range(8):
        k, half = divmod(j, 2)
        at = (slice(half * 32, half * 32 + 32), slice(k * 128, (k + 1) * 128))
        result[at] = whole[j] - weight[at]

    settle(before_whole, count[0])


def publish(
    result, grad_weight, grad_lane, grad_supplier, grad_region, grad_company, grad_scale
):
    grad_weight[...] = result[:, 0:512]
    pair = result[:, 512:640]
    grad_lane[...] = pair[:, 0:64]
    grad_region[...] = pair[:, 64:128]
    rest = result[:, 640:768]
    grad_supplier[...] = rest[0:32, 0:64]
    grad_company[...] = rest[32:40, 0:64]
    grad_scale[...] = rest[40:44, 0:64]


def per_device(
    covariates,
    weight,
    scale,
    z_lane,
    z_supplier,
    z_region,
    z_company,
    group_owner,
    group_local,
    group_len,
    event_bin,
    observed,
    lane_supplier,
    supplier_region,
    region_company,
):
    vmem = pl.BlockSpec(memory_space=pltpu.VMEM)
    hbm = pl.BlockSpec(memory_space=pltpu.HBM)
    operands = (
        covariates,
        weight.T,
        scale,
        z_lane,
        z_supplier,
        z_region,
        z_company,
        group_owner.reshape(1, 64),
        group_local.reshape(1, 64),
        group_len.reshape(1, 64),
        event_bin.reshape(16, 128),
        observed.reshape(16, 128),
        lane_supplier.reshape(1, 64),
        supplier_region.reshape(32, 128),
        region_company.reshape(1, 64),
    )
    shapes = ((64, 512), (64, 64), (32, 64), (64, 64), (8, 64), (4, 64))
    shapes = tuple(jax.ShapeDtypeStruct(shape, F) for shape in shapes)
    slots = 224
    result = pl.pallas_call(
        kernel,
        out_shape=pltpu.VMEM((64, 768), F),
        in_specs=[hbm] * 15,
        out_specs=vmem,
        scratch_shapes=[pltpu.VMEM(op.shape, op.dtype) for op in operands[1:]]
        + [
            pltpu.VMEM((4, ROWS, 128), B),
            pltpu.VMEM((64, ROWS), F),
            pltpu.VMEM((64, ROWS), B),
            pltpu.VMEM((16, 48, 128), S),
            pltpu.VMEM((16, 1, 128), F),
            pltpu.VMEM((8, 1, 128), F),
            pltpu.VMEM((8, 8, 128), F),
            pltpu.VMEM((16, 1, 128), F),
            pltpu.VMEM((8, 32, 128), S),
            pltpu.VMEM((8, 32, 128), S),
            pltpu.VMEM((8, 32, 128), S),
            pltpu.VMEM((8, 32, 128), S),
            pltpu.VMEM((16, 32, 128), B),
            pltpu.VMEM((8, 32, 128), B),
            pltpu.VMEM((8, 32, 128), B),
            pltpu.VMEM((16, 32, 128), B),
            pltpu.VMEM((16, 1, 128), F),
            pltpu.VMEM((8, 1, 128), F),
            pltpu.VMEM((8, 80, 128), B),
            pltpu.VMEM((8, 80, 128), B),
            pltpu.VMEM((8, 32, 128), F),
            pltpu.SemaphoreType.DMA((CHUNKS,)),
            pltpu.SemaphoreType.DMA((14,)),
            pltpu.SemaphoreType.DMA((slots,)),
            pltpu.SemaphoreType.DMA((slots,)),
        ],
        compiler_params=pltpu.CompilerParams(
            collective_id=0, has_side_effects=True, vmem_limit_bytes=VMEM_BYTES
        ),
        name="hazard_gradient",
    )(*operands)
    results = pl.pallas_call(
        publish,
        out_shape=shapes,
        in_specs=[vmem],
        out_specs=tuple(pl.BlockSpec(shape.shape, lambda: (0, 0)) for shape in shapes),
        name="publish",
    )(pltpu.with_memory_space_constraint(result, pltpu.VMEM))
    return (results[0].T,) + tuple(results[1:])


def solution(mesh):
    in_specs = (
        P("dp", "mp"),
        P(None, "mp"),
        P(None, "mp"),
        P("dp", "mp"),
        P("dp", "mp"),
        P(None, "mp"),
        P(None, "mp"),
        P("dp", None),
        P("dp"),
        P("dp"),
        P("dp"),
        P("dp"),
        P("dp"),
        P(),
        P(),
    )
    out_specs = (
        P(None, "mp"),
        P("dp", "mp"),
        P("dp", "mp"),
        P(None, "mp"),
        P(None, "mp"),
        P(None, "mp"),
    )
    return jax.shard_map(
        per_device, mesh=mesh, in_specs=in_specs, out_specs=out_specs, check_vma=False
    )
```

```python
import jax
import jax.numpy as jnp
from jax import lax
from jax.experimental import pallas as pl
from jax.experimental.pallas import tpu as pltpu
from jax.sharding import PartitionSpec as P

HIGHEST = lax.Precision.HIGHEST
F = jnp.float32
B = jnp.bfloat16
I = jnp.int32
S = jnp.int16
VMEM_BYTES = 60 * 1024 * 1024
CHUNKS = 8
ROWS = 2048
CH = ROWS // CHUNKS
HALF = CH // 2
STEPS = (8, 7, 9, 6, 10, 5, 11, 4, 12, 3, 13, 2, 14, 1, 15)
UNIT = 5461.0


def iota(shape, axis):
    return lax.broadcasted_iota(I, shape, axis)


def mm(a, b, ca=1, cb=0, precision=None):
    return lax.dot_general(
        a, b, (((ca,), (cb,)), ((), ())), preferred_element_type=F, precision=precision
    )


def pick(cond, dtype=F):
    return jnp.where(cond, jnp.float32(1.0), jnp.float32(0.0)).astype(dtype)


def column(row):
    n = row.shape[1]
    return jnp.sum(
        jnp.where(iota((n, n), 0) == iota((n, n), 1), row, jnp.zeros_like(row)),
        axis=1,
        keepdims=True,
    )


def row_of(col):
    n = col.shape[0]
    return jnp.sum(
        jnp.where(iota((n, n), 0) == iota((n, n), 1), col, jnp.zeros_like(col)),
        axis=0,
        keepdims=True,
    )


def side(a, b):
    return jnp.concatenate([a, b], axis=1)


def fixed(value):
    return jnp.floor(value * UNIT + 0.5).astype(I)


def stack(value, rows):
    return jnp.concatenate([value[:rows, 0:64], value[:rows, 64:128]], axis=0)


def fold(value):
    half = value.shape[0] // 2
    return side(value[:half, :], value[half:, :])


def kernel(*refs):
    hbm = refs[:15]
    result = refs[15]
    held_in = refs[16:30]
    (
        covers,
        linear,
        scores,
        nodes,
        lane_ids,
        group_ids,
        found_ids,
        row_ids,
        reply,
        replied,
        sup_reply,
        sup_replied,
        sums,
        parts,
        part_in,
        weight_in,
        scale_rows,
        scale_in,
        parted,
        parted_in,
        whole,
        local_sem,
        load_sem,
        send_sem,
        recv_sem,
    ) = refs[30:]
    cov = hbm[0]
    (
        weight,
        scale,
        z_lane,
        z_supplier,
        z_region,
        z_company,
        group_owner,
        group_local,
        group_len,
        event_bin,
        observed,
        lane_supplier,
        supplier_region,
        region_company,
    ) = held_in
    dp = lax.axis_index("dp")
    mp = lax.axis_index("mp")
    z = lax.div(dp, 8)
    yc = lax.rem(dp, 8)
    right = lax.rem(mp + 1, 4)
    left = lax.rem(mp + 3, 4)

    def at_z(step):
        return {"dp": lax.rem(z + step, 16) * 8 + yc, "mp": mp}

    def at_yc(step):
        return {"dp": z * 8 + lax.rem(yc + step, 8), "mp": mp}

    def at_x(index):
        return {"dp": dp, "mp": index}

    barrier = pltpu.get_barrier_semaphore()
    partners = [at_z(step) for step in STEPS]
    partners += [at_yc(step) for step in range(1, 8)]
    partners += [at_x(right), at_x(left)]
    for device in partners:
        pl.semaphore_signal(
            barrier, inc=1, device_id=device, device_id_type=pl.DeviceIdType.MESH
        )

    loads = []
    for k in range(14):
        copy = pltpu.make_async_copy(hbm[k + 1], held_in[k], load_sem.at[k])
        copy.start()
        loads.append(copy)

    own_copies = []
    for c in range(CHUNKS):
        rows = pl.ds(c * CH, CH)
        copy = pltpu.make_async_copy(cov.at[rows], covers.at[mp, rows], local_sem.at[c])
        copy.start()
        own_copies.append(copy)

    count = [0]
    started = []

    def send(src, dst, device):
        slot = count[0]
        count[0] = slot + 1
        copy = pltpu.make_async_remote_copy(
            src_ref=src,
            dst_ref=dst,
            send_sem=send_sem.at[slot],
            recv_sem=recv_sem.at[slot],
            device_id=device,
            device_id_type=pl.DeviceIdType.MESH,
        )
        copy.start()
        started.append(copy)
        return copy

    def settle(first, last):
        for copy in started[first:last]:
            copy.wait_send()

    def arrive(copies):
        for copy in copies:
            copy.wait_recv()

    def along_z(buf):
        return [send(buf.at[z], buf.at[z], at_z(step)) for step in STEPS]

    def plane(buf):
        return [send(buf.at[yc], buf.at[yc], at_yc(step)) for step in range(1, 8)]

    def scatter(source, target):
        return [
            send(source.at[lax.rem(yc + step, 8)], target.at[yc], at_yc(step))
            for step in range(1, 8)
        ]

    direct = {}
    passed = {}

    def launch(c):
        rows = pl.ds(c * CH, CH)
        block = covers.at[mp, rows]
        direct[c] = [
            send(cov.at[rows], block, at_x(right)),
            send(cov.at[rows], block, at_x(left)),
        ]

    def forward(c):
        arrive(direct[c])
        first = covers.at[left, pl.ds(c * CH, HALF)]
        second = covers.at[right, pl.ds(c * CH + HALF, HALF)]
        passed[c] = [send(first, first, at_x(right)), send(second, second, at_x(left))]

    for copy in loads:
        copy.wait()
    own_owner = group_owner[...].astype(F)
    own_local = group_local[...].astype(F)
    nodes[z, 0:32, :] = fold(fixed(z_lane[...])).astype(S)
    nodes[z, 32:48, :] = fold(fixed(z_supplier[...])).astype(S)
    of_lane = lane_supplier[...]
    lane_ids[z] = side(of_lane >> 6, of_lane & 63).astype(F)
    group_ids[yc] = side(own_owner, own_local)
    pl.semaphore_wait(barrier, len(partners))

    for c in range(2):
        launch(c)
    lane_id_copies = along_z(lane_ids)
    group_id_copies = plane(group_ids)
    for c in range(2, 4):
        launch(c)
    node_copies = along_z(nodes)
    for c in range(4, CHUNKS):
        launch(c)

    weight_rows = weight[...].astype(B)
    company_effect = scale[0:1, :] * z_company[...]
    companies = region_company[...]
    company_pick = pick(iota((64, 8), 1) == column(companies.astype(F)).astype(I))
    region_effect = scale[1:2, :] * z_region[...] + mm(
        company_pick, company_effect, precision=HIGHEST
    )
    lens = group_len[...].astype(F)
    spread = jnp.where(
        (iota((16, 64), 1) >> 2) == iota((16, 64), 0), lens, jnp.zeros_like(lens)
    )
    lanes_of = pick((iota((64, 128), 0) & 3) == (iota((64, 128), 1) >> 5), B)
    live_len = mm(spread.astype(B), lanes_of).astype(I)
    ends = jnp.where((iota((16, 128), 1) & 31) < live_len, event_bin[...], -1)
    flags = observed[...].astype(F)

    arrive(group_id_copies)
    ids = jnp.concatenate([group_ids[j] for j in range(8)], axis=0).astype(I)
    owners, locals_ = ids[:, 0:64], ids[:, 64:128]
    held = jnp.where((owners & 7) == yc, owners >> 3, -1)
    lane_key = jnp.where(held >= 0, held * 64 + locals_, -1)
    lane_columns = [
        column(lane_key[j : j + 1, :].astype(F)).astype(I) for j in range(8)
    ]

    def flat(rows):
        return jnp.concatenate([rows[j : j + 1, :] for j in range(8)], axis=1)

    owner_pick = pick(iota((16, 512), 0) == flat(held), B)
    local_pick = iota((64, 512), 0) == flat(locals_)
    forward(0)
    forward(1)
    forward(2)

    arrive(lane_id_copies)
    table = jnp.concatenate([lane_ids[k] for k in range(16)], axis=0).T.astype(B)
    of_owner = mm(table, owner_pick)
    of_owner = of_owner[0:64, :] * 64.0 + of_owner[64:128, :]
    found = jnp.sum(jnp.where(local_pick, of_owner, jnp.float32(0.0)), axis=0, keepdims=True)
    found = jnp.concatenate([found[:, j * 64 : j * 64 + 64] for j in range(8)], axis=0)
    found_ids[yc] = side(found, jnp.zeros((8, 64), F))
    found_copies = plane(found_ids)
    forward(3)
    forward(4)

    def digits(first, size):
        value = nodes[:, first : first + size, :].reshape(16 * size, 128).astype(I)
        high = (value + 64) >> 7
        low = value - (high << 7)
        return side(high.astype(F).astype(B), low.astype(F).astype(B))

    def chosen(row, upper, table):
        got = mm(pick(iota((64, table.shape[0]), 1) == row, B), table)
        got = got[:, 0:128] * 128.0 + got[:, 128:256]
        return jnp.where(upper, got[:, 64:128], got[:, 0:64])

    arrive(node_copies)
    lane_table = digits(0, 32)
    for j in range(8):
        key = lane_columns[j]
        row = jnp.where(key >= 0, (key >> 6) * 32 + (key & 31), -1)
        reply[j] = fold(chosen(row, (key & 32) > 0, lane_table)).astype(I).astype(S)
    replied[yc] = reply[yc]
    reply_copies = scatter(reply, replied)
    forward(5)

    arrive(found_copies)
    suppliers = found_ids[0]
    for j in range(1, 8):
        suppliers = suppliers + found_ids[j]
    suppliers = suppliers[:, 0:64]
    own_supplier = jnp.sum(
        jnp.where(iota((8, 64), 0) == yc, suppliers, jnp.float32(0.0)), axis=0, keepdims=True
    )
    suppliers = suppliers.astype(I)
    sup_table = digits(32, 16)
    sup_key = jnp.where(((suppliers >> 5) & 7) == yc, suppliers, -1)
    for j in range(8):
        key = column(sup_key[j : j + 1, :].astype(F)).astype(I)
        row = jnp.where(key >= 0, (key >> 8) * 16 + (key & 15), -1)
        sup_reply[j] = fold(chosen(row, (key & 16) > 0, sup_table)).astype(I).astype(S)
    sup_replied[yc] = sup_reply[yc]
    reply_copies += scatter(sup_reply, sup_replied)
    forward(6)

    own_sup_col = column(own_supplier).astype(I)
    sup_row = pick(iota((64, 32), 1) == (own_sup_col >> 7), B)
    region_table = mm(sup_row, supplier_region[...].astype(F).astype(B))
    group_region = jnp.sum(
        jnp.where(iota((64, 128), 1) == (own_sup_col & 127), region_table, jnp.float32(0.0)),
        axis=1,
        keepdims=True,
    )
    region_col = group_region.astype(I)
    row_ids[z] = side(
        own_supplier * 64.0 + row_of(group_region), own_owner * 64.0 + own_local
    )
    row_id_copies = along_z(row_ids)
    group_effect = mm(
        pick(iota((64, 64), 1) == region_col), region_effect, precision=HIGHEST
    )
    forward(7)

    def covered(first, last):
        return jnp.concatenate([covers[k, first * CH : last * CH, :] for k in range(4)], axis=1)

    def project(c):
        own_copies[c].wait()
        arrive(passed[c])
        linear[:, c * CH : (c + 1) * CH] = mm(weight_rows, covered(c, c + 1), 1, 1)

    for c in range(6):
        project(c)

    arrive(reply_copies)

    def latent(buf):
        got = buf[0].astype(I)
        for j in range(1, 8):
            got = got + buf[j].astype(I)
        return stack(got.astype(F) * (1.0 / UNIT), 32)

    lane_latent, sup_latent = latent(replied), latent(sup_replied)
    path = scale[2:3, :] * sup_latent + group_effect
    offset = (scale[3:4, :] * lane_latent + path).astype(B)
    offset = offset.astype(F).T.astype(B)

    for c in range(6, CHUNKS):
        project(c)
    bins = iota((64, 128), 0) + mp * 64

    def score_block(s):
        at = slice(s * 128, (s + 1) * 128)
        expand = pick(iota((64, 128), 0) == (iota((64, 128), 1) >> 5) + 4 * s, B)
        eta = linear[:, at] + mm(offset, expand)
        hazard = jax.nn.sigmoid(eta)
        end = ends[s : s + 1, :]
        score = jnp.where(
            bins < end,
            -hazard,
            jnp.where(bins == end, flags[s : s + 1, :] - hazard, jnp.float32(0.0)),
        )
        scores[:, at] = score.astype(B)

    for block in range(16):
        score_block(block)
    group_pick = pick(iota((64, 2048), 0) == (iota((64, 2048), 1) >> 5), B)
    group_sum = mm(group_pick, scores[...], 1, 1)
    sums[z] = fold(group_sum).astype(B)
    sum_copies = along_z(sums)

    product = None
    for first in range(0, CHUNKS, 2):
        part = mm(scores[:, first * CH : (first + 2) * CH], covered(first, first + 2))
        product = part if product is None else product + part
    for j in range(8):
        k, half = divmod(j, 2)
        block = product[half * 32 : half * 32 + 32, k * 128 : (k + 1) * 128]
        parts[j] = block.astype(B)
    part_in[yc] = parts[yc]
    before_parts = count[0]
    part_copies = scatter(parts, part_in)

    scale_rows[z] = side(
        jnp.sum(lane_latent * group_sum, axis=0, keepdims=True),
        jnp.sum(sup_latent * group_sum, axis=0, keepdims=True),
    )
    scale_copies = along_z(scale_rows)

    def added(buf, many):
        total = buf[0].astype(F)
        for k in range(1, many):
            total = total + buf[k].astype(F)
        return total

    arrive(part_copies)
    weight_in[z] = added(part_in, 8).astype(B)
    weight_copies = along_z(weight_in)

    arrive(row_id_copies)
    held_rows = jnp.concatenate([row_ids[k] for k in range(16)], axis=0).astype(I)

    def along(start):
        return jnp.concatenate(
            [held_rows[k : k + 1, start : start + 32] for k in range(16)], axis=1
        )

    sup_along = side(along(0), along(32))
    region_along = sup_along & 63
    sup_along = (sup_along >> 6) - z * 256
    lane_along = side(along(64), along(96)) - z * 512
    lane_hit = pick(iota((512, 1024), 0) == lane_along, B)
    sup_hit = pick(iota((256, 1024), 0) == sup_along, B)
    region_hit = pick(iota((64, 1024), 0) == region_along, B)

    arrive(sum_copies)
    gathered = stack(sums[...].reshape(512, 128), 512)
    by_lane = mm(lane_hit, gathered)
    by_supplier = mm(sup_hit, gathered)
    by_region = fold(mm(region_hit, gathered)).astype(B)
    for j in range(8):
        parted[j, 0:32, :] = fold(by_lane[j * 64 : j * 64 + 64, :]).astype(B)
        parted[j, 32:48, :] = fold(by_supplier[j * 32 : j * 32 + 32, :]).astype(B)
        parted[j, 48:80, :] = by_region
    parted_in[yc] = parted[yc]
    lane_copies = scatter(parted, parted_in)
    arrive(scale_copies)
    scale_in[yc] = added(scale_rows, 16)
    scale_copies = plane(scale_in)

    settle(0, before_parts)
    arrive(weight_copies)
    whole[yc] = added(weight_in, 16)
    before_whole = count[0]
    whole_copies = plane(whole)

    arrive(lane_copies)
    total = added(parted_in, 8)
    grad_lane = scale[3:4, :] * stack(total, 32) - z_lane[...]
    grad_supplier = scale[2:3, :] * stack(total[32:48, :], 16) - z_supplier[...]
    region_total = stack(total[48:80, :], 32)
    result[0:32, 640:768] = side(grad_supplier, jnp.zeros((32, 64), F))
    arrive(scale_copies)
    scale_total = added(scale_in, 8)
    company_total = mm(
        pick(iota((8, 64), 0) == companies), region_total, precision=HIGHEST
    )
    grad_region = scale[1:2, :] * region_total - z_region[...]
    grad_company = scale[0:1, :] * company_total - z_company[...]
    result[:, 512:640] = side(grad_lane, grad_region)
    result[32:40, 640:768] = side(grad_company, jnp.zeros((8, 64), F))
    of_company = jnp.sum(z_company[...] * company_total, axis=0, keepdims=True)
    of_region = jnp.sum(z_region[...] * region_total, axis=0, keepdims=True)
    rank = iota((8, 64), 0)
    grad_scale = jnp.where(
        rank == 0,
        of_company,
        jnp.where(
            rank == 1,
            of_region,
            jnp.where(rank == 2, scale_total[:, 64:128], scale_total[:, 0:64]),
        ),
    )
    result[40:48, 640:768] = side(grad_scale, jnp.zeros((8, 64), F))
    result[48:64, 640:768] = jnp.zeros((16, 128), F)

    settle(before_parts, before_whole)
    arrive(whole_copies)
    for j in range(8):
        k, half = divmod(j, 2)
        at = (slice(half * 32, half * 32 + 32), slice(k * 128, (k + 1) * 128))
        result[at] = whole[j] - weight[at]

    settle(before_whole, count[0])


def publish(
    result, grad_weight, grad_lane, grad_supplier, grad_region, grad_company, grad_scale
):
    grad_weight[...] = result[:, 0:512]
    pair = result[:, 512:640]
    grad_lane[...] = pair[:, 0:64]
    grad_region[...] = pair[:, 64:128]
    rest = result[:, 640:768]
    grad_supplier[...] = rest[0:32, 0:64]
    grad_company[...] = rest[32:40, 0:64]
    grad_scale[...] = rest[40:44, 0:64]


def per_device(
    covariates,
    weight,
    scale,
    z_lane,
    z_supplier,
    z_region,
    z_company,
    group_owner,
    group_local,
    group_len,
    event_bin,
    observed,
    lane_supplier,
    supplier_region,
    region_company,
):
    vmem = pl.BlockSpec(memory_space=pltpu.VMEM)
    hbm = pl.BlockSpec(memory_space=pltpu.HBM)
    operands = (
        covariates,
        weight.T,
        scale,
        z_lane,
        z_supplier,
        z_region,
        z_company,
        group_owner.reshape(1, 64),
        group_local.reshape(1, 64),
        group_len.reshape(1, 64),
        event_bin.reshape(16, 128),
        observed.reshape(16, 128),
        lane_supplier.reshape(1, 64),
        supplier_region.reshape(32, 128),
        region_company.reshape(1, 64),
    )
    shapes = ((64, 512), (64, 64), (32, 64), (64, 64), (8, 64), (4, 64))
    shapes = tuple(jax.ShapeDtypeStruct(shape, F) for shape in shapes)
    slots = 224
    result = pl.pallas_call(
        kernel,
        out_shape=pltpu.VMEM((64, 768), F),
        in_specs=[hbm] * 15,
        out_specs=vmem,
        scratch_shapes=[pltpu.VMEM(op.shape, op.dtype) for op in operands[1:]]
        + [
            pltpu.VMEM((4, ROWS, 128), B),
            pltpu.VMEM((64, ROWS), F),
            pltpu.VMEM((64, ROWS), B),
            pltpu.VMEM((16, 48, 128), S),
            pltpu.VMEM((16, 1, 128), F),
            pltpu.VMEM((8, 1, 128), F),
            pltpu.VMEM((8, 8, 128), F),
            pltpu.VMEM((16, 1, 128), F),
            pltpu.VMEM((8, 32, 128), S),
            pltpu.VMEM((8, 32, 128), S),
            pltpu.VMEM((8, 32, 128), S),
            pltpu.VMEM((8, 32, 128), S),
            pltpu.VMEM((16, 32, 128), B),
            pltpu.VMEM((8, 32, 128), B),
            pltpu.VMEM((8, 32, 128), B),
            pltpu.VMEM((16, 32, 128), B),
            pltpu.VMEM((16, 1, 128), F),
            pltpu.VMEM((8, 1, 128), F),
            pltpu.VMEM((8, 80, 128), B),
            pltpu.VMEM((8, 80, 128), B),
            pltpu.VMEM((8, 32, 128), F),
            pltpu.SemaphoreType.DMA((CHUNKS,)),
            pltpu.SemaphoreType.DMA((14,)),
            pltpu.SemaphoreType.DMA((slots,)),
            pltpu.SemaphoreType.DMA((slots,)),
        ],
        compiler_params=pltpu.CompilerParams(
            collective_id=0, has_side_effects=True, vmem_limit_bytes=VMEM_BYTES
        ),
        name="hazard_gradient",
    )(*operands)
    results = pl.pallas_call(
        publish,
        out_shape=shapes,
        in_specs=[vmem],
        out_specs=tuple(pl.BlockSpec(shape.shape, lambda: (0, 0)) for shape in shapes),
        name="publish",
    )(pltpu.with_memory_space_constraint(result, pltpu.VMEM))
    return (results[0].T,) + tuple(results[1:])


def solution(mesh):
    in_specs = (
        P("dp", "mp"),
        P(None, "mp"),
        P(None, "mp"),
        P("dp", "mp"),
        P("dp", "mp"),
        P(None, "mp"),
        P(None, "mp"),
        P("dp", None),
        P("dp"),
        P("dp"),
        P("dp"),
        P("dp"),
        P("dp"),
        P(),
        P(),
    )
    out_specs = (
        P(None, "mp"),
        P("dp", "mp"),
        P("dp", "mp"),
        P(None, "mp"),
        P(None, "mp"),
        P(None, "mp"),
    )
    return jax.shard_map(
        per_device, mesh=mesh, in_specs=in_specs, out_specs=out_specs, check_vma=False
    )
```
